32 devices in a mesh: groups: 2 (over y), tiles: 4 (over z), sub: 2 (over x), adj: 2 (over core).
Axes of the slice: x: 2, y: 2, z: 4, core: 2. Of those that a mesh axis runs over, the one named last changes fastest.
Arguments:
- innovation: float32 [128, 256], P(('groups', 'tiles'), 'sub'), parts along dimension 0, may hold values from -6 to 6
- cluster: int32 [128, 256], P(('groups', 'tiles'), 'sub'), parts along dimension 0, may hold values from 0 to 8
- kernel: float32 [36, 64, 256], P(None, 'tiles', 'sub'), may hold values from 0.2 to 1.5
- wind_x: float32 [36, 64, 256], P(None, 'tiles', 'sub'), may hold values from -0.24 to 0.24
- wind_y: float32 [36, 64, 256], P(None, 'tiles', 'sub'), may hold values from -0.24 to 0.24
- conv_strength: float32 [64, 256], P('tiles', 'sub'), may hold values from 0 to 0.9
- conv_matrix: float32 [36, 36], replicated, may hold values from 0 to 1, as said below
- margin_cell: int32 [6144, 8], P(('tiles', 'sub')), may hold values from 0 to 16383, as said below
- margin_weight: float32 [6144, 8], P(('tiles', 'sub')), may hold values from 0 to 1, as said below
Outputs:
- adjoint_field: float32 [16, 36, 64, 256], P(('groups', 'adj'), None, 'tiles', 'sub'), parts along dimension 0
- sensitivity: float32 [16, 6144], P(('groups', 'adj'), ('tiles', 'sub')), parts along dimension 0
The draws below stay inside these ranges and needn't reach their ends.
There are 2 independent parts, one for each index of `groups`. The reference program is written for one: setup_inputs(seed, part) draws one part's arguments, and reference() takes and returns one part's arrays. A program takes and returns all parts, laid end to end along the dimension named above; an argument that names none is the same for every part. Nothing has to cross between parts.
Inputs may be any that keep to these rules, and one draw needn't show every extreme that they name: `conv_matrix`: entries are positive and every column sums to 1. `margin_cell`: state element e is owned by block b = e // 768, with t = b // 2 and s = b % 2; the column index of each of its cells lies in t * 16 - 16 to t * 16 + 2 * 16 - 1, taken modulo 64, and its row in s * 128 - 128 to s * 128 + 2 * 128 - 1 (within 0 to 255). `margin_weight`: each state element has 1 to 8 live slots first, element 0 all 8; the others have weight 0.
All inputs are finite; a program needn't handle non-finite values.
Results may differ from the reference program's by a relative error of at most 0.0003.
Values sent between devices are 32-bit elements; how exact they have to be, the bound alone decides.
A program may use at most 64 MiB of HBM per device.

```python
import jax
import jax.numpy as jnp
from jax import lax

ADJ = 8
LEV = 36
NSTEP = 2
KOV = 8
CX = 16
CY = 128
E_DEV = 768
NX = 64
NY = 256
NE = 6144
N_SUB = 2


def margin_tables(key):
    folded = jax.random.fold_in(key, 11)
    subkeys = jax.random.split(folded, 5)
    element = jnp.arange(NE, dtype=jnp.int32)
    owner_block = element // E_DEV
    tile_block = owner_block // N_SUB
    cross_block = owner_block % N_SUB
    live_count = jax.random.randint(subkeys[0], (NE,), 1, KOV + 1)
    live_count = jnp.where(element == 0, KOV, live_count)
    shift_x = jax.random.randint(subkeys[1], (NE, KOV), -CX, 2 * CX)
    column_x = (tile_block[:, None] * CX + shift_x + NX) % NX
    low_y = jnp.maximum(cross_block * CY - CY, 0)
    high_y = jnp.minimum(cross_block * CY + 2 * CY, NY)
    row_y = jax.random.randint(subkeys[2], (NE, KOV), low_y[:, None], high_y[:, None])
    cells = (column_x * NY + row_y).astype(jnp.int32)
    live_slot = jnp.arange(KOV)[None, :] < live_count[:, None]
    weights = jax.random.uniform(subkeys[4], (NE, KOV), jnp.float32, 0.2, 1.0) * live_slot.astype(jnp.float32)
    return (cells, weights)


def draw_margin_cell(key, part):
    return margin_tables(key)[0]


def draw_margin_weight(key, part):
    return margin_tables(key)[1]


def draw_conv_matrix(key, part):
    folded = jax.random.fold_in(key, 23)
    spread = jnp.exp(jax.random.uniform(folded, (LEV, LEV), jnp.float32, -2.0, 1.5))
    mixing = spread / jnp.sum(spread, axis=0, keepdims=True)
    return 0.4 * jnp.eye(LEV, dtype=jnp.float32) + 0.6 * mixing


def plant(values, rng, smallest, top_value):
    index_at = [jax.random.randint(jax.random.fold_in(rng, axis), (), 0, length) for axis, length in enumerate(values.shape)]
    longest = values.shape.index(max(values.shape))
    beside = index_at[:longest] + [(index_at[longest] + 1) % values.shape[longest]] + index_at[longest + 1:]
    return values.at[tuple(index_at)].set(smallest).at[tuple(beside)].set(top_value)


def levels(own_key, dims, shards, low, high):
    loudness = 1.0
    for axis_at, shards_of in shards:
        heights = jax.random.uniform(jax.random.fold_in(jax.random.fold_in(own_key, 6), axis_at), (shards_of,), jnp.float32, low / len(shards), high / len(shards))
        loudness = loudness * jnp.repeat(jnp.exp(heights), dims[axis_at] // shards_of).reshape((-1,) + (1,) * (len(dims) - 1 - axis_at))
    return loudness


def scatter_about(stream_key, dims, deviation, most, cuts=(), kind=jnp.bfloat16):
    values = deviation * jax.random.normal(stream_key, dims, jnp.float32)
    if cuts:
        values = values * levels(stream_key, dims, cuts, -0.22, 0.18)
    return jnp.clip(values, -most, most).astype(kind)


def setup_inputs(seed: int = 0, part: int = 0) -> dict:
    key_list = jax.random.split(jax.random.key(seed), 10)
    own_keys = jax.random.split(jax.random.fold_in(key_list[9], part), 10)
    innovation = scatter_about(own_keys[0], (NX, NY), 1.0, 6.0, ((0, 4), (1, 2)), jnp.float32)
    cluster = plant(jax.random.randint(own_keys[1], (NX, NY), 0, ADJ + 1), jax.random.fold_in(own_keys[1], 1), 0, ADJ).astype(jnp.int32)
    kernel = jnp.clip(0.2 + 1.3 * jax.random.uniform(key_list[2], (LEV, NX, NY), jnp.float32) ** levels(key_list[2], (LEV, NX, NY), ((1, 4), (2, 2)), -0.2, 0.2), 0.2, 1.5)
    wind_x = jnp.clip(jax.random.uniform(key_list[3], (LEV, NX, NY), jnp.float32, -0.24, 0.24) * levels(key_list[3], (LEV, NX, NY), ((1, 4), (2, 2)), -0.4, 0.0), -0.24, 0.24)
    wind_y = jnp.clip(jax.random.uniform(key_list[4], (LEV, NX, NY), jnp.float32, -0.24, 0.24) * levels(key_list[4], (LEV, NX, NY), ((1, 4), (2, 2)), -0.4, 0.0), -0.24, 0.24)
    conv_strength = jnp.clip(0.9 * jax.random.uniform(key_list[5], (NX, NY), jnp.float32) ** levels(key_list[5], (NX, NY), ((0, 4), (1, 2)), -0.2, 0.2), 0.0, 0.9)
    conv_matrix = draw_conv_matrix(jax.random.fold_in(key_list[9], 71), part)
    margin_cell = draw_margin_cell(jax.random.fold_in(key_list[9], 71), part)
    margin_weight = draw_margin_weight(jax.random.fold_in(key_list[9], 71), part)
    return {"innovation": innovation, "cluster": cluster, "kernel": kernel, "wind_x": wind_x, "wind_y": wind_y, "conv_strength": conv_strength, "conv_matrix": conv_matrix, "margin_cell": margin_cell, "margin_weight": margin_weight}


def transport(adjoint, wind_x, wind_y):
    east_rate = jnp.maximum(wind_x, 0.0)
    west_rate = jnp.minimum(jnp.roll(wind_x, 1, axis=1), 0.0)
    north_rate = jnp.maximum(wind_y, 0.0)
    south_rate = jnp.pad(jnp.minimum(wind_y[:, :, :-1], 0.0), ((0, 0), (0, 0), (1, 0)))
    east = jnp.roll(adjoint, -1, axis=1)
    west = jnp.roll(adjoint, 1, axis=1)
    north = jnp.pad(adjoint[:, :, 1:], ((0, 0), (0, 0), (0, 1)))
    south = jnp.pad(adjoint[:, :, :-1], ((0, 0), (0, 0), (1, 0)))
    center = 1.0 - east_rate + west_rate - north_rate + south_rate
    return adjoint * center + east_rate * east - west_rate * west + north_rate * north - south_rate * south


def convect(adjoint, strength, matrix):
    mixed = jnp.einsum("lk,lxy->kxy", matrix, adjoint, precision=lax.Precision.HIGHEST)
    return adjoint + strength * (mixed - adjoint)


def reference(innovation, cluster, kernel, wind_x, wind_y, conv_strength, conv_matrix, margin_cell, margin_weight):
    def single(index):
        adjoint = jnp.where(cluster == index, innovation, 0.0)[None] * kernel
        for step in range(NSTEP):
            adjoint = convect(adjoint, conv_strength, conv_matrix)
            adjoint = transport(adjoint, wind_x, wind_y)
        surface = adjoint[0].reshape(-1)
        values = surface[margin_cell]
        return adjoint, jnp.sum(margin_weight * values, axis=1)

    field, sensed = lax.map(single, jnp.arange(ADJ, dtype=jnp.int32))
    return (field, sensed)
```

```python
import functools

import jax
import jax.numpy as jnp
from jax import lax
from jax.experimental import pallas as pl
from jax.experimental.pallas import tpu as pltpu
from jax.sharding import PartitionSpec as P

ADJ = 8
NSTEP = 2
MESH = pl.DeviceIdType.MESH


def offsets(count):
    return [0, 1, -1][: min(3, count)]


def slot_of(offset, count):
    return offset % min(3, count)


def divmod_const(value, number):
    if number & (number - 1) == 0:
        return value >> (number.bit_length() - 1), value & (number - 1)
    return value // number, value % number


def split(value):
    high = value.astype(jnp.bfloat16).astype(jnp.float32)
    return high, value - high


def stacked(value, depth):
    high, low = split(value)
    rows, lanes = value.shape
    parts = [high, low, high]
    if depth > 3 * rows:
        parts.append(jnp.zeros((depth - 3 * rows, lanes), jnp.float32))
    return jnp.concatenate(parts, axis=0).astype(jnp.bfloat16)


def kernel_body(
    dims,
    innovation,
    cluster,
    kernel,
    wind_x,
    wind_y,
    strength,
    matrix,
    cells,
    weights,
    field,
    sensed,
    base,
    face_x,
    south_rates,
    pack_a,
    pack_b,
    state,
    table,
    square,
    send_sem,
    recv_sem,
):
    levels, width, adjoints, n_t, n_s = dims
    padded = base.shape[1]
    lanes = base.shape[2]
    depth = square.shape[0]
    me_g = lax.axis_index("groups")
    me_t = lax.axis_index("tiles")
    me_s = lax.axis_index("sub")
    me_a = lax.axis_index("adj")
    nx, ny = min(3, n_t), min(3, n_s)

    def device(dt, ds):
        return (me_g, lax.rem(me_t + dt + n_t, n_t), lax.rem(me_s + ds + n_s, n_s), me_a)

    partners = [(dt, ds) for dt in offsets(n_t) for ds in offsets(n_s) if (dt, ds) != (0, 0)]
    barrier = pltpu.get_barrier_semaphore()
    for dt, ds in partners:
        pl.semaphore_signal(barrier, inc=1, device_id=device(dt, ds), device_id_type=MESH)

    count = [0]

    def send(src, dst, dt, ds):
        at = count[0]
        count[0] += 1
        copy = pltpu.make_async_remote_copy(
            src_ref=src,
            dst_ref=dst,
            send_sem=send_sem.at[at],
            recv_sem=recv_sem.at[at],
            device_id=device(dt, ds),
            device_id_type=MESH,
        )
        copy.start()
        return copy

    square[...] = jnp.zeros_like(square)
    square[0:levels, 0:levels] = matrix[...]
    high, low = split(square[...].T)
    mixer = high + pltpu.roll(high, padded, 1) + pltpu.roll(low, 2 * padded, 1)
    mixer = mixer[0:padded].astype(jnp.bfloat16)

    def mix(value):
        return jnp.dot(mixer, stacked(value, depth), preferred_element_type=jnp.float32)

    lane = lax.broadcasted_iota(jnp.int32, (padded, lanes), 1)
    pair = ((lane + 1) & (lanes - 1)) >> 1
    level = lax.broadcasted_iota(jnp.int32, (padded, lanes), 0)

    last = padded - 8

    def prepare(x, packed):
        rows = pl.ds(x, levels, stride=width)
        empty = jnp.zeros((8, lanes), jnp.float32)
        face_x[1 + x, last:padded, :] = empty
        south_rates[x, last:padded, :] = empty
        base[1 + x, last:padded, :] = empty
        face_x[1 + x, 0:levels, :] = wind_x[rows, :]
        south_rates[x, 0:levels, :] = wind_y[rows, :]
        base[1 + x, 0:levels, :] = kernel[rows, :]
        column = base[1 + x]
        one = pl.ds(x, 1)
        mixed = mix(column)
        column = (column + strength[one, :] * (mixed - column)) * innovation[one, :]
        column = jnp.where(level == levels, cluster[one, :].astype(jnp.float32), column)
        base[1 + x] = column
        packed = jnp.where(pair == x, pltpu.roll(column, 2 * x, 1), packed)
        faces = south_rates[x]
        packed = jnp.where(pair == width + x, pltpu.roll(faces, 2 * (width + x), 1), packed)
        return packed

    packed = jnp.zeros((padded, lanes), jnp.float32)
    packed = lax.fori_loop(0, width, prepare, packed)
    pack_a[0] = packed

    pl.semaphore_wait(barrier, len(partners))

    def send_pack(pack):
        return [
            send(pack.at[0], pack.at[slot_of(-ds, n_s)], 0, ds) for ds in offsets(n_s) if ds != 0
        ]

    copies = send_pack(pack_a)
    copies.append(send(base.at[1], base.at[width + 1], -1, 0))
    copies.append(send(base.at[width], base.at[0], 1, 0))
    copies.append(send(face_x.at[width], face_x.at[0], 1, 0))
    for copy in copies:
        copy.wait()

    odd = (lane & 1) == 1
    has_south = jnp.where(me_s > 0, 1.0, 0.0)
    has_north = jnp.where(me_s < n_s - 1, 1.0, 0.0)

    def merged(pack):
        south = pltpu.roll(pack[slot_of(-1, n_s)], 2, 1) * has_south
        north = pack[slot_of(1, n_s)] * has_north
        return jnp.where(odd, south, north)

    def edges(pack, at, value):
        seam = pltpu.roll(pack, lanes - 1 - 2 * at, 1)
        rows = lane[0 : value.shape[0]]
        north = jnp.where(rows == lanes - 1, seam, pltpu.roll(value, lanes - 1, 1))
        south = jnp.where(rows == 0, seam, pltpu.roll(value, 1, 1))
        return north, south

    seam_a = merged(pack_a)
    first_id = (me_a * adjoints).astype(jnp.float32)

    def advance(x, packed):
        face_y = south_rates[x]
        _, face_south = edges(seam_a, width + x, face_y)
        east_rate = jnp.maximum(face_x[1 + x], 0.0)
        west_rate = jnp.minimum(face_x[x], 0.0)
        north_rate = jnp.maximum(face_y, 0.0)
        south_rate = jnp.minimum(face_south, 0.0)
        center_rate = 1.0 - east_rate + west_rate - north_rate + south_rate
        center, east, west = base[1 + x], base[2 + x], base[x]
        north, south = edges(seam_a, x, center)
        terms = [
            (center * center_rate, center),
            (east * east_rate, east),
            (-west * west_rate, west),
            (north * north_rate, north),
            (-south * south_rate, south),
        ]
        values = []
        for a in range(adjoints):
            total = None
            for product, source in terms:
                ids = source[levels : levels + 1, :]
                chosen = jnp.where(ids == first_id + a, 1.0, 0.0)
                part = product * chosen
                total = part if total is None else total + part
            values.append(total)
        together = jnp.concatenate(values, axis=1)
        mixed = mix(together)
        fraction = strength[pl.ds(x, 1), :]
        for a in range(adjoints):
            value = values[a]
            value = value + fraction * (mixed[:, a * lanes : (a + 1) * lanes] - value)
            state[1 + x, a] = value
            at = a * width + x
            packed = jnp.where(pair == at, pltpu.roll(value, 2 * at, 1), packed)
        return packed

    packed = jnp.zeros((padded, lanes), jnp.float32)
    packed = advance(0, packed)
    packed = advance(width - 1, packed)
    copies = [
        send(state.at[1], state.at[width + 1], -1, 0),
        send(state.at[width], state.at[0], 1, 0),
    ]
    packed = lax.fori_loop(1, width - 1, advance, packed)
    pack_b[0] = packed
    copies += send_pack(pack_b)
    for copy in copies:
        copy.wait()
    seam_b = merged(pack_b)

    def transport(x, low, high):
        face_y = south_rates[x, low:high]
        _, face_south = edges(seam_a[low:high], width + x, face_y)
        east_rate = jnp.maximum(face_x[1 + x, low:high], 0.0)
        west_rate = jnp.minimum(face_x[x, low:high], 0.0)
        north_rate = jnp.maximum(face_y, 0.0)
        south_rate = jnp.minimum(face_south, 0.0)
        center_rate = 1.0 - east_rate + west_rate - north_rate + south_rate
        results = []
        for a in range(adjoints):
            center = state[1 + x, a, low:high]
            north, south = edges(seam_b[low:high], a * width + x, center)
            results.append(
                center * center_rate
                + east_rate * state[2 + x, a, low:high]
                - west_rate * state[x, a, low:high]
                + north_rate * north
                - south_rate * south
            )
        return results

    first = 8

    def surface(x, carry):
        for a, value in enumerate(transport(x, 0, first)):
            field[pl.ds(a * levels * width + x, first, stride=width), :] = value
            table[0, pl.ds(a * width + x, 1), :] = value[0:1, :]
        return carry

    lax.fori_loop(0, width, surface, 0)
    copies = []
    for dt, ds in partners:
        slot = slot_of(dt, n_t) * ny + slot_of(ds, n_s)
        there = slot_of(-dt, n_t) * ny + slot_of(-ds, n_s)
        copies.append(send(table.at[0], table.at[there], dt, ds))

    def rest(x, carry):
        for a, value in enumerate(transport(x, first, padded)):
            rows = pl.ds((a * levels + first) * width + x, levels - first, stride=width)
            field[rows, :] = value[0 : levels - first, :]
        return carry

    lax.fori_loop(0, width, rest, 0)

    column, row = divmod_const(cells[...], n_s * lanes)
    tile, in_tile = divmod_const(column, width)
    block, in_block = divmod_const(row, lanes)
    step_t = tile - me_t
    step_t = jnp.where(step_t < 0, step_t + n_t, step_t)
    step_t = jnp.where(step_t > 1, 2, step_t)
    step_s = block - me_s
    step_s = jnp.where(step_s < 0, step_s + ny, step_s)
    table_row = (step_t * ny + step_s) * width + in_tile
    elements = cells.shape[1]
    chunks = elements // lanes
    slots = cells.shape[0]

    for copy in copies:
        copy.wait()

    def pick(at, carry):
        slot, x = divmod_const(at, width)
        taken = list(carry)
        masks = [table_row[:, c * lanes : (c + 1) * lanes] == at for c in range(chunks)]
        for a in range(adjoints):
            line = jnp.broadcast_to(table[slot, pl.ds(a * width + x, 1), :], (slots, lanes))
            for c in range(chunks):
                found = jnp.take_along_axis(
                    line, in_block[:, c * lanes : (c + 1) * lanes], axis=1, mode="promise_in_bounds"
                )
                i = a * chunks + c
                taken[i] = jnp.where(masks[c], found, taken[i])
        return tuple(taken)

    empty = jnp.zeros((slots, lanes), jnp.float32)
    taken = lax.fori_loop(0, nx * ny * width, pick, (empty,) * (adjoints * chunks))
    for a in range(adjoints):
        for c in range(chunks):
            part = taken[a * chunks + c] * weights[:, c * lanes : (c + 1) * lanes]
            sensed[a : a + 1, c * lanes : (c + 1) * lanes] = jnp.sum(part, axis=0, keepdims=True)


def body(
    innovation,
    cluster,
    kernel,
    wind_x,
    wind_y,
    conv_strength,
    conv_matrix,
    margin_cell,
    margin_weight,
):
    levels, width, lanes = kernel.shape
    n_t, n_s = lax.axis_size("tiles"), lax.axis_size("sub")
    adjoints = ADJ // lax.axis_size("adj")
    elements, slots = margin_cell.shape
    padded = 8 * (levels // 8 + 1)
    depth = 128 * pl.cdiv(3 * padded, 128)
    nx, ny = min(3, n_t), min(3, n_s)
    n_sems = 2 * (ny - 1) + 5 + nx * ny - 1
    vmem = pl.BlockSpec(memory_space=pltpu.VMEM)
    field, sensed = pl.pallas_call(
        functools.partial(kernel_body, (levels, width, adjoints, n_t, n_s)),
        out_shape=(
            jax.ShapeDtypeStruct((adjoints * levels * width, lanes), jnp.float32),
            jax.ShapeDtypeStruct((adjoints, elements), jnp.float32),
        ),
        in_specs=[vmem] * 9,
        out_specs=(vmem, vmem),
        scratch_shapes=[
            pltpu.VMEM((width + 2, padded, lanes), jnp.float32),
            pltpu.VMEM((width + 2, padded, lanes), jnp.float32),
            pltpu.VMEM((width, padded, lanes), jnp.float32),
            pltpu.VMEM((ny, padded, lanes), jnp.float32),
            pltpu.VMEM((ny, padded, lanes), jnp.float32),
            pltpu.VMEM((width + 2, adjoints, padded, lanes), jnp.float32),
            pltpu.VMEM((nx * ny, adjoints * width, lanes), jnp.float32),
            pltpu.VMEM((depth, depth), jnp.float32),
            pltpu.SemaphoreType.DMA((n_sems,)),
            pltpu.SemaphoreType.DMA((n_sems,)),
        ],
        compiler_params=pltpu.CompilerParams(
            collective_id=0, has_side_effects=True, vmem_limit_bytes=48 * 1024 * 1024
        ),
    )(
        innovation,
        cluster,
        kernel.reshape(levels * width, lanes),
        wind_x.reshape(levels * width, lanes),
        wind_y.reshape(levels * width, lanes),
        conv_strength,
        conv_matrix,
        margin_cell.T,
        margin_weight.T,
    )
    return field.reshape(adjoints, levels, width, lanes), sensed


def solution(mesh):
    in_specs = (
        P(("groups", "tiles"), "sub"),
        P(("groups", "tiles"), "sub"),
        P(None, "tiles", "sub"),
        P(None, "tiles", "sub"),
        P(None, "tiles", "sub"),
        P("tiles", "sub"),
        P(),
        P(("tiles", "sub"), None),
        P(("tiles", "sub"), None),
    )
    out_specs = (P(("groups", "adj"), None, "tiles", "sub"), P(("groups", "adj"), ("tiles", "sub")))
    return jax.shard_map(body, mesh=mesh, in_specs=in_specs, out_specs=out_specs, check_vma=False)
```

```python
import functools

import jax
import jax.numpy as jnp
from jax import lax
from jax.experimental import pallas as pl
from jax.experimental.pallas import tpu as pltpu
from jax.sharding import PartitionSpec as P

ADJ = 8
NSTEP = 2
MESH = pl.DeviceIdType.MESH


def offsets(count):
    return [0, 1, -1][: min(3, count)]


def slot_of(offset, count):
    return offset % min(3, count)


def divmod_const(value, number):
    if number & (number - 1) == 0:
        return value >> (number.bit_length() - 1), value & (number - 1)
    return value // number, value % number


def split(value):
    high = value.astype(jnp.bfloat16).astype(jnp.float32)
    return high, value - high


def stacked(value, depth):
    high, low = split(value)
    rows, lanes = value.shape
    parts = [high, low, high]
    if depth > 3 * rows:
        parts.append(jnp.zeros((depth - 3 * rows, lanes), jnp.float32))
    return jnp.concatenate(parts, axis=0).astype(jnp.bfloat16)


def kernel_body(
    dims,
    *refs,
):
    sources, (field, sensed), scratch = refs[:9], refs[9:11], refs[11:]
    arrivals, scratch = scratch[:9], scratch[9:]
    innovation, cluster, kernel, wind_x, wind_y, strength, matrix, cells, weights = arrivals
    (
        base,
        face_x,
        south_rates,
        pack_a,
        pack_b,
        state,
        table,
        square,
        send_sem,
        recv_sem,
        load_sem,
    ) = scratch
    levels, width, adjoints, n_t, n_s = dims
    padded = base.shape[1]
    lanes = base.shape[2]
    depth = square.shape[0]
    me_g = lax.axis_index("groups")
    me_t = lax.axis_index("tiles")
    me_s = lax.axis_index("sub")
    me_a = lax.axis_index("adj")
    nx, ny = min(3, n_t), min(3, n_s)

    def device(dt, ds):
        return (me_g, lax.rem(me_t + dt + n_t, n_t), lax.rem(me_s + ds + n_s, n_s), me_a)

    partners = [(dt, ds) for dt in offsets(n_t) for ds in offsets(n_s) if (dt, ds) != (0, 0)]
    barrier = pltpu.get_barrier_semaphore()
    for dt, ds in partners:
        pl.semaphore_signal(barrier, inc=1, device_id=device(dt, ds), device_id_type=MESH)
    loads = [
        pltpu.make_async_copy(source, arrival, load_sem.at[i])
        for i, (source, arrival) in enumerate(zip(sources, arrivals))
    ]
    for i in (6, 2, 0, 1, 5, 3, 4, 7, 8):
        loads[i].start()

    count = [0]

    def send(src, dst, dt, ds):
        at = count[0]
        count[0] += 1
        copy = pltpu.make_async_remote_copy(
            src_ref=src,
            dst_ref=dst,
            send_sem=send_sem.at[at],
            recv_sem=recv_sem.at[at],
            device_id=device(dt, ds),
            device_id_type=MESH,
        )
        copy.start()
        return copy

    square[...] = jnp.zeros_like(square)
    loads[6].wait()
    square[0:levels, 0:levels] = matrix[...]
    high, low = split(square[...].T)
    mixer = high + pltpu.roll(high, padded, 1) + pltpu.roll(low, 2 * padded, 1)
    mixer = mixer[0:padded].astype(jnp.bfloat16)

    def mix(value):
        return jnp.dot(mixer, stacked(value, depth), preferred_element_type=jnp.float32)

    lane = lax.broadcasted_iota(jnp.int32, (padded, lanes), 1)
    pair = ((lane + 1) & (lanes - 1)) >> 1
    level = lax.broadcasted_iota(jnp.int32, (padded, lanes), 0)

    last = padded - 8

    for load in loads[:6]:
        load.wait()

    def prepare(x, packed):
        rows = pl.ds(x, levels, stride=width)
        empty = jnp.zeros((8, lanes), jnp.float32)
        face_x[1 + x, last:padded, :] = empty
        south_rates[x, last:padded, :] = empty
        base[1 + x, last:padded, :] = empty
        face_x[1 + x, 0:levels, :] = wind_x[rows, :]
        south_rates[x, 0:levels, :] = wind_y[rows, :]
        base[1 + x, 0:levels, :] = kernel[rows, :]
        column = base[1 + x]
        one = pl.ds(x, 1)
        mixed = mix(column)
        column = (column + strength[one, :] * (mixed - column)) * innovation[one, :]
        column = jnp.where(level == levels, cluster[one, :].astype(jnp.float32), column)
        base[1 + x] = column
        packed = jnp.where(pair == x, pltpu.roll(column, 2 * x, 1), packed)
        faces = south_rates[x]
        packed = jnp.where(pair == width + x, pltpu.roll(faces, 2 * (width + x), 1), packed)
        return packed

    def send_pack(pack):
        return [
            send(pack.at[0], pack.at[slot_of(-ds, n_s)], 0, ds) for ds in offsets(n_s) if ds != 0
        ]

    packed = jnp.zeros((padded, lanes), jnp.float32)
    packed = prepare(0, packed)
    packed = prepare(width - 1, packed)
    pl.semaphore_wait(barrier, len(partners))
    copies = [
        send(face_x.at[width], face_x.at[0], 1, 0),
        send(base.at[width], base.at[0], 1, 0),
        send(base.at[1], base.at[width + 1], -1, 0),
    ]
    packed = lax.fori_loop(1, width - 1, prepare, packed, unroll=True)
    pack_a[0] = packed
    copies += send_pack(pack_a)
    for copy in copies:
        copy.wait()

    odd = (lane & 1) == 1
    has_south = jnp.where(me_s > 0, 1.0, 0.0)
    has_north = jnp.where(me_s < n_s - 1, 1.0, 0.0)

    def merged(pack):
        south = pltpu.roll(pack[slot_of(-1, n_s)], 2, 1) * has_south
        north = pack[slot_of(1, n_s)] * has_north
        return jnp.where(odd, south, north)

    def edges(pack, at, value):
        seam = pltpu.roll(pack, lanes - 1 - 2 * at, 1)
        rows = lane[0 : value.shape[0]]
        north = jnp.where(rows == lanes - 1, seam, pltpu.roll(value, lanes - 1, 1))
        south = jnp.where(rows == 0, seam, pltpu.roll(value, 1, 1))
        return north, south

    seam_a = merged(pack_a)
    first_id = (me_a * adjoints).astype(jnp.float32)

    def advance(x, packed):
        face_y = south_rates[x]
        _, face_south = edges(seam_a, width + x, face_y)
        east_rate = jnp.maximum(face_x[1 + x], 0.0)
        west_rate = jnp.minimum(face_x[x], 0.0)
        north_rate = jnp.maximum(face_y, 0.0)
        south_rate = jnp.minimum(face_south, 0.0)
        center_rate = 1.0 - east_rate + west_rate - north_rate + south_rate
        center, east, west = base[1 + x], base[2 + x], base[x]
        north, south = edges(seam_a, x, center)
        terms = [
            (center * center_rate, center),
            (east * east_rate, east),
            (-west * west_rate, west),
            (north * north_rate, north),
            (-south * south_rate, south),
        ]
        values = []
        for a in range(adjoints):
            total = None
            for product, source in terms:
                ids = source[levels : levels + 1, :]
                chosen = jnp.where(ids == first_id + a, 1.0, 0.0)
                part = product * chosen
                total = part if total is None else total + part
            values.append(total)
        together = jnp.concatenate(values, axis=1)
        mixed = mix(together)
        fraction = strength[pl.ds(x, 1), :]
        for a in range(adjoints):
            value = values[a]
            value = value + fraction * (mixed[:, a * lanes : (a + 1) * lanes] - value)
            state[1 + x, a] = value
            at = a * width + x
            packed = jnp.where(pair == at, pltpu.roll(value, 2 * at, 1), packed)
        return packed

    packed = jnp.zeros((padded, lanes), jnp.float32)
    packed = advance(0, packed)
    packed = advance(width - 1, packed)
    copies = [
        send(state.at[1], state.at[width + 1], -1, 0),
        send(state.at[width], state.at[0], 1, 0),
    ]
    packed = lax.fori_loop(1, width - 1, advance, packed, unroll=True)
    pack_b[0] = packed
    copies += send_pack(pack_b)
    for copy in copies:
        copy.wait()
    seam_b = merged(pack_b)

    def transport(x, low, high):
        face_y = south_rates[x, low:high]
        _, face_south = edges(seam_a[low:high], width + x, face_y)
        east_rate = jnp.maximum(face_x[1 + x, low:high], 0.0)
        west_rate = jnp.minimum(face_x[x, low:high], 0.0)
        north_rate = jnp.maximum(face_y, 0.0)
        south_rate = jnp.minimum(face_south, 0.0)
        center_rate = 1.0 - east_rate + west_rate - north_rate + south_rate
        results = []
        for a in range(adjoints):
            center = state[1 + x, a, low:high]
            north, south = edges(seam_b[low:high], a * width + x, center)
            results.append(
                center * center_rate
                + east_rate * state[2 + x, a, low:high]
                - west_rate * state[x, a, low:high]
                + north_rate * north
                - south_rate * south
            )
        return results

    first = 8

    def surface(x, carry):
        for a, value in enumerate(transport(x, 0, first)):
            field[pl.ds(a * levels * width + x, first, stride=width), :] = value
            table[0, pl.ds(a * width + x, 1), :] = value[0:1, :]
        return carry

    lax.fori_loop(0, width, surface, 0, unroll=True)
    copies = []
    for dt, ds in partners:
        slot = slot_of(dt, n_t) * ny + slot_of(ds, n_s)
        there = slot_of(-dt, n_t) * ny + slot_of(-ds, n_s)
        copies.append(send(table.at[0], table.at[there], dt, ds))

    def rest(x, carry):
        for a, value in enumerate(transport(x, first, padded)):
            rows = pl.ds((a * levels + first) * width + x, levels - first, stride=width)
            field[rows, :] = value[0 : levels - first, :]
        return carry

    lax.fori_loop(0, width, rest, 0, unroll=True)

    loads[7].wait()
    loads[8].wait()
    column, row = divmod_const(cells[...], n_s * lanes)
    tile, in_tile = divmod_const(column, width)
    block, in_block = divmod_const(row, lanes)
    step_t = tile - me_t
    step_t = jnp.where(step_t < 0, step_t + n_t, step_t)
    step_t = jnp.where(step_t > 1, 2, step_t)
    step_s = block - me_s
    step_s = jnp.where(step_s < 0, step_s + ny, step_s)
    table_row = (step_t * ny + step_s) * width + in_tile
    elements = cells.shape[1]
    chunks = elements // lanes
    slots = cells.shape[0]

    for copy in copies:
        copy.wait()

    def pick(at, carry):
        slot, x = divmod_const(at, width)
        taken = list(carry)
        masks = [table_row[:, c * lanes : (c + 1) * lanes] == at for c in range(chunks)]
        for a in range(adjoints):
            line = jnp.broadcast_to(table[slot, pl.ds(a * width + x, 1), :], (slots, lanes))
            for c in range(chunks):
                found = jnp.take_along_axis(
                    line, in_block[:, c * lanes : (c + 1) * lanes], axis=1, mode="promise_in_bounds"
                )
                i = a * chunks + c
                taken[i] = jnp.where(masks[c], found, taken[i])
        return tuple(taken)

    empty = jnp.zeros((slots, lanes), jnp.float32)
    taken = lax.fori_loop(0, nx * ny * width, pick, (empty,) * (adjoints * chunks), unroll=4)
    for a in range(adjoints):
        for c in range(chunks):
            part = taken[a * chunks + c] * weights[:, c * lanes : (c + 1) * lanes]
            sensed[a : a + 1, c * lanes : (c + 1) * lanes] = jnp.sum(part, axis=0, keepdims=True)


def body(
    innovation,
    cluster,
    kernel,
    wind_x,
    wind_y,
    conv_strength,
    conv_matrix,
    margin_cell,
    margin_weight,
):
    levels, width, lanes = kernel.shape
    n_t, n_s = lax.axis_size("tiles"), lax.axis_size("sub")
    adjoints = ADJ // lax.axis_size("adj")
    elements, slots = margin_cell.shape
    padded = 8 * (levels // 8 + 1)
    depth = 128 * pl.cdiv(3 * padded, 128)
    nx, ny = min(3, n_t), min(3, n_s)
    n_sems = 2 * (ny - 1) + 5 + nx * ny - 1
    vmem = pl.BlockSpec(memory_space=pltpu.VMEM)
    operands = (
        innovation,
        cluster,
        kernel.reshape(levels * width, lanes),
        wind_x.reshape(levels * width, lanes),
        wind_y.reshape(levels * width, lanes),
        conv_strength,
        conv_matrix,
        margin_cell.T,
        margin_weight.T,
    )
    field, sensed = pl.pallas_call(
        functools.partial(kernel_body, (levels, width, adjoints, n_t, n_s)),
        out_shape=(
            jax.ShapeDtypeStruct((adjoints * levels * width, lanes), jnp.float32),
            jax.ShapeDtypeStruct((adjoints, elements), jnp.float32),
        ),
        in_specs=[pl.BlockSpec(memory_space=pltpu.HBM)] * 9,
        out_specs=(vmem, vmem),
        scratch_shapes=[pltpu.VMEM(x.shape, x.dtype) for x in operands]
        + [
            pltpu.VMEM((width + 2, padded, lanes), jnp.float32),
            pltpu.VMEM((width + 2, padded, lanes), jnp.float32),
            pltpu.VMEM((width, padded, lanes), jnp.float32),
            pltpu.VMEM((ny, padded, lanes), jnp.float32),
            pltpu.VMEM((ny, padded, lanes), jnp.float32),
            pltpu.VMEM((width + 2, adjoints, padded, lanes), jnp.float32),
            pltpu.VMEM((nx * ny, adjoints * width, lanes), jnp.float32),
            pltpu.VMEM((depth, depth), jnp.float32),
            pltpu.SemaphoreType.DMA((n_sems,)),
            pltpu.SemaphoreType.DMA((n_sems,)),
            pltpu.SemaphoreType.DMA((len(operands),)),
        ],
        compiler_params=pltpu.CompilerParams(
            collective_id=0, has_side_effects=True, vmem_limit_bytes=60 * 1024 * 1024
        ),
    )(*operands)
    return field.reshape(adjoints, levels, width, lanes), sensed


def solution(mesh):
    in_specs = (
        P(("groups", "tiles"), "sub"),
        P(("groups", "tiles"), "sub"),
        P(None, "tiles", "sub"),
        P(None, "tiles", "sub"),
        P(None, "tiles", "sub"),
        P("tiles", "sub"),
        P(),
        P(("tiles", "sub"), None),
        P(("tiles", "sub"), None),
    )
    out_specs = (P(("groups", "adj"), None, "tiles", "sub"), P(("groups", "adj"), ("tiles", "sub")))
    return jax.shard_map(body, mesh=mesh, in_specs=in_specs, out_specs=out_specs, check_vma=False)
```

```python
import functools

import jax
import jax.numpy as jnp
from jax import lax
from jax.experimental import pallas as pl
from jax.experimental.pallas import tpu as pltpu
from jax.sharding import PartitionSpec as P

ADJ = 8
NSTEP = 2
MESH = pl.DeviceIdType.MESH


def offsets(count):
    return [0, 1, -1][: min(3, count)]


def slot_of(offset, count):
    return offset % min(3, count)


def divmod_const(value, number):
    if number & (number - 1) == 0:
        return value >> (number.bit_length() - 1), value & (number - 1)
    return value // number, value % number


def split(value):
    high = value.astype(jnp.bfloat16).astype(jnp.float32)
    return high, value - high


def stacked(value, depth):
    high, low = split(value)
    rows, lanes = value.shape
    parts = [high, low, high]
    if depth > 3 * rows:
        parts.append(jnp.zeros((depth - 3 * rows, lanes), jnp.float32))
    return jnp.concatenate(parts, axis=0).astype(jnp.bfloat16)


def kernel_body(
    dims,
    *refs,
):
    sources, (field, surfaces), scratch = refs[:7], refs[7:9], refs[9:]
    arrivals, scratch = scratch[:7], scratch[7:]
    innovation, cluster, kernel, wind_x, wind_y, strength, matrix = arrivals
    (
        base,
        face_x,
        face_y,
        pack_a,
        pack_b,
        state,
        table,
        held,
        square,
        send_sem,
        recv_sem,
        load_sem,
        store_sem,
    ) = scratch
    levels, width, adjoints, n_t, n_s = dims
    padded = base.shape[1]
    lanes = base.shape[2]
    depth = square.shape[0]
    me_g = lax.axis_index("groups")
    me_t = lax.axis_index("tiles")
    me_s = lax.axis_index("sub")
    me_a = lax.axis_index("adj")
    nx, ny = min(3, n_t), min(3, n_s)

    def device(dt, ds):
        return (me_g, lax.rem(me_t + dt + n_t, n_t), lax.rem(me_s + ds + n_s, n_s), me_a)

    partners = [(dt, ds) for dt in offsets(n_t) for ds in offsets(n_s) if (dt, ds) != (0, 0)]
    barrier = pltpu.get_barrier_semaphore()
    for dt, ds in partners:
        pl.semaphore_signal(barrier, inc=1, device_id=device(dt, ds), device_id_type=MESH)
    loads = [
        pltpu.make_async_copy(source, arrival, load_sem.at[i])
        for i, (source, arrival) in enumerate(zip(sources, arrivals))
    ]
    for i in (6, 2, 0, 1, 5, 3, 4):
        loads[i].start()

    count = [0]

    def send(src, dst, dt, ds):
        at = count[0]
        count[0] += 1
        copy = pltpu.make_async_remote_copy(
            src_ref=src,
            dst_ref=dst,
            send_sem=send_sem.at[at],
            recv_sem=recv_sem.at[at],
            device_id=device(dt, ds),
            device_id_type=MESH,
        )
        copy.start()
        return copy

    square[...] = jnp.zeros_like(square)
    loads[6].wait()
    square[0:levels, 0:levels] = matrix[...]
    high, low = split(square[...].T)
    mixer = high + pltpu.roll(high, padded, 1) + pltpu.roll(low, 2 * padded, 1)
    mixer = mixer[0:padded].astype(jnp.bfloat16)

    def mix(value):
        return jnp.dot(mixer, stacked(value, depth), preferred_element_type=jnp.float32)

    lane = lax.broadcasted_iota(jnp.int32, (padded, lanes), 1)
    pair = ((lane + 1) & (lanes - 1)) >> 1
    level = lax.broadcasted_iota(jnp.int32, (padded, lanes), 0)

    last = levels // 8 * 8
    for load in loads[:6]:
        load.wait()

    def prepare(x, packed):
        rows = pl.ds(x, levels, stride=width)
        empty = jnp.zeros((padded - last, lanes), jnp.float32)
        face_x[2 + x, last:padded, :] = empty
        face_y[1 + x, last:padded, :] = empty
        base[2 + x, last:padded, :] = empty
        face_x[2 + x, 0:levels, :] = wind_x[rows, :]
        face_y[1 + x, 0:levels, :] = wind_y[rows, :]
        base[2 + x, 0:levels, :] = kernel[rows, :]
        column = base[2 + x]
        one = pl.ds(x, 1)
        mixed = mix(column)
        column = (column + strength[one, :] * (mixed - column)) * innovation[one, :]
        column = jnp.where(level == levels, cluster[one, :].astype(jnp.float32), column)
        column = jnp.where(level == levels + 1, strength[one, :], column)
        base[2 + x] = column
        packed = jnp.where(pair == x, pltpu.roll(column, 2 * x, 1), packed)
        faces = face_y[1 + x]
        packed = jnp.where(pair == width + x, pltpu.roll(faces, 2 * (width + x), 1), packed)
        return packed

    packed = jnp.zeros((padded, lanes), jnp.float32)
    for x in (0, 1, width - 2, width - 1):
        packed = prepare(x, packed)
    pl.semaphore_wait(barrier, len(partners))
    copies_x = [
        send(base.at[pl.ds(width, 2)], base.at[pl.ds(0, 2)], 1, 0),
        send(base.at[pl.ds(2, 2)], base.at[pl.ds(width + 2, 2)], -1, 0),
        send(face_x.at[pl.ds(width, 2)], face_x.at[pl.ds(0, 2)], 1, 0),
        send(face_x.at[2], face_x.at[width + 2], -1, 0),
        send(face_y.at[width], face_y.at[0], 1, 0),
        send(face_y.at[1], face_y.at[width + 1], -1, 0),
    ]
    packed = lax.fori_loop(2, width - 2, prepare, packed, unroll=True)
    pack_a[0] = packed
    near, far = [], []
    for dt, ds in partners:
        if ds != 0:
            there = slot_of(-dt, n_t) * ny + slot_of(-ds, n_s)
            copy = send(pack_a.at[0], pack_a.at[there], dt, ds)
            (far if dt else near).append(copy)
    for copy in near:
        copy.wait()

    odd = (lane & 1) == 1
    has_south = jnp.where(me_s > 0, 1.0, 0.0)
    has_north = jnp.where(me_s < n_s - 1, 1.0, 0.0)

    def merged(pack, dt):
        row = slot_of(dt, n_t) * ny
        south = pltpu.roll(pack[row + slot_of(-1, n_s)], 2, 1) * has_south
        north = pack[row + slot_of(1, n_s)] * has_north
        return jnp.where(odd, south, north)

    def edges(pack, at, value):
        seam = pltpu.roll(pack, lanes - 1 - 2 * at, 1)
        rows = lane[0 : value.shape[0]]
        north = jnp.where(rows == lanes - 1, seam, pltpu.roll(value, lanes - 1, 1))
        south = jnp.where(rows == 0, seam, pltpu.roll(value, 1, 1))
        return north, south

    seam_a = merged(pack_a, 0)
    first_id = (me_a * adjoints).astype(jnp.float32)

    def advance(x, seam, at):
        flow_y = face_y[1 + x]
        _, flow_south = edges(seam, width + at, flow_y)
        east_rate = jnp.maximum(face_x[2 + x], 0.0)
        west_rate = jnp.minimum(face_x[1 + x], 0.0)
        north_rate = jnp.maximum(flow_y, 0.0)
        south_rate = jnp.minimum(flow_south, 0.0)
        center_rate = 1.0 - east_rate + west_rate - north_rate + south_rate
        center, east, west = base[2 + x], base[3 + x], base[1 + x]
        north, south = edges(seam, at, center)
        terms = [
            (center * center_rate, center),
            (east * east_rate, east),
            (-west * west_rate, west),
            (north * north_rate, north),
            (-south * south_rate, south),
        ]
        values = []
        for a in range(adjoints):
            total = None
            for product, source in terms:
                ids = source[levels : levels + 1, :]
                chosen = jnp.where(ids == first_id + a, 1.0, 0.0)
                part = product * chosen
                total = part if total is None else total + part
            values.append(total)
        mixed = mix(jnp.concatenate(values, axis=1))
        fraction = center[levels + 1 : levels + 2, :]
        results = []
        for a in range(adjoints):
            value = values[a]
            value = value + fraction * (mixed[:, a * lanes : (a + 1) * lanes] - value)
            state[1 + x, a] = value
            results.append(value)
        return results

    def inside(x, packed):
        for a, value in enumerate(advance(x, seam_a, x)):
            at = a * width + x
            packed = jnp.where(pair == at, pltpu.roll(value, 2 * at, 1), packed)
        return packed

    packed = jnp.zeros((padded, lanes), jnp.float32)
    packed = lax.fori_loop(1, width - 1, inside, packed, unroll=True)
    for copy in copies_x:
        copy.wait()
    packed = inside(0, packed)
    packed = inside(width - 1, packed)
    pack_b[0] = packed
    copies = [
        send(pack_b.at[0], pack_b.at[slot_of(-ds, n_s)], 0, ds) for ds in offsets(n_s) if ds != 0
    ]
    for copy in far:
        copy.wait()
    advance(-1, merged(pack_a, -1), width - 1)
    advance(width, merged(pack_a, 1), 0)
    for copy in copies:
        copy.wait()
    seam_b = merged(pack_b, 0)

    stores = []

    def transport(low, high):
        top = min(high, levels)

        def along(x, carry):
            flow_y = face_y[1 + x, low:high]
            _, flow_south = edges(seam_a[low:high], width + x, flow_y)
            east_rate = jnp.maximum(face_x[2 + x, low:high], 0.0)
            west_rate = jnp.minimum(face_x[1 + x, low:high], 0.0)
            north_rate = jnp.maximum(flow_y, 0.0)
            south_rate = jnp.minimum(flow_south, 0.0)
            center_rate = 1.0 - east_rate + west_rate - north_rate + south_rate
            for a in range(adjoints):
                center = state[1 + x, a, low:high]
                north, south = edges(seam_b[low:high], a * width + x, center)
                value = (
                    center * center_rate
                    + east_rate * state[2 + x, a, low:high]
                    - west_rate * state[x, a, low:high]
                    + north_rate * north
                    - south_rate * south
                )
                rows = pl.ds((a * levels + low) * width + x, top - low, stride=width)
                held[rows, :] = value[0 : top - low, :]
                if low == 0:
                    table[0, pl.ds(a * width + x, 1), :] = value[0:1, :]
            return carry

        lax.fori_loop(0, width, along, 0, unroll=True)

    def store(low, high):
        top = min(high, levels)
        for a in range(adjoints):
            rows = pl.ds((a * levels + low) * width, (top - low) * width)
            copy = pltpu.make_async_copy(held.at[rows], field.at[rows], store_sem.at[len(stores)])
            copy.start()
            stores.append(copy)

    transport(0, 8)
    copies = []
    for dt, ds in partners:
        there = slot_of(-dt, n_t) * ny + slot_of(-ds, n_s)
        copies.append(send(table.at[0], table.at[there], dt, ds))
    store(0, 8)
    for low in range(8, padded, 8):
        transport(low, low + 8)
        store(low, low + 8)
    for copy in copies:
        copy.wait()
    own = pltpu.make_async_copy(table, surfaces, store_sem.at[len(stores)])
    own.start()
    for copy in stores:
        copy.wait()
    own.wait()


def gather_body(dims, cells, weights, surfaces, field, field_out, sensed, table, copy_sem, table_sem):
    width, adjoints, n_t, n_s = dims
    lanes = table.shape[2]
    nx, ny = min(3, n_t), min(3, n_s)
    me_t = lax.axis_index("tiles")
    me_s = lax.axis_index("sub")
    arrival = pltpu.make_async_copy(surfaces, table, table_sem)
    arrival.start()
    share = field.shape[0] // adjoints
    copies = []
    for a in range(adjoints):
        rows = pl.ds(a * share, share)
        copy = pltpu.make_async_copy(field.at[rows], field_out.at[rows], copy_sem.at[a])
        copy.start()
        copies.append(copy)

    column, row = divmod_const(cells[...], n_s * lanes)
    tile, in_tile = divmod_const(column, width)
    block, in_block = divmod_const(row, lanes)
    step_t = tile - me_t
    step_t = jnp.where(step_t < 0, step_t + n_t, step_t)
    step_t = jnp.where(step_t > 1, 2, step_t)
    step_s = block - me_s
    step_s = jnp.where(step_s < 0, step_s + ny, step_s)
    table_row = (step_t * ny + step_s) * width + in_tile
    elements = cells.shape[1]
    chunks = elements // lanes
    slots = cells.shape[0]

    arrival.wait()

    def pick(at, carry):
        slot, x = divmod_const(at, width)
        taken = list(carry)
        masks = [table_row[:, c * lanes : (c + 1) * lanes] == at for c in range(chunks)]
        for a in range(adjoints):
            line = jnp.broadcast_to(table[slot, pl.ds(a * width + x, 1), :], (slots, lanes))
            for c in range(chunks):
                found = jnp.take_along_axis(
                    line, in_block[:, c * lanes : (c + 1) * lanes], axis=1, mode="promise_in_bounds"
                )
                i = a * chunks + c
                taken[i] = jnp.where(masks[c], found, taken[i])
        return tuple(taken)

    empty = jnp.zeros((slots, lanes), jnp.float32)
    taken = lax.fori_loop(0, nx * ny * width, pick, (empty,) * (adjoints * chunks), unroll=4)
    for a in range(adjoints):
        for c in range(chunks):
            part = taken[a * chunks + c] * weights[:, c * lanes : (c + 1) * lanes]
            sensed[a : a + 1, c * lanes : (c + 1) * lanes] = jnp.sum(part, axis=0, keepdims=True)
    for copy in copies:
        copy.wait()


def body(
    innovation,
    cluster,
    kernel,
    wind_x,
    wind_y,
    conv_strength,
    conv_matrix,
    margin_cell,
    margin_weight,
):
    levels, width, lanes = kernel.shape
    n_t, n_s = lax.axis_size("tiles"), lax.axis_size("sub")
    adjoints = ADJ // lax.axis_size("adj")
    elements, slots = margin_cell.shape
    padded = 8 * pl.cdiv(levels + 2, 8)
    depth = 128 * pl.cdiv(3 * padded, 128)
    nx, ny = min(3, n_t), min(3, n_s)
    n_sems = 6 + 2 * (nx * ny - 1) - (nx - 1) + ny - 1
    anywhere = pl.BlockSpec(memory_space=pl.ANY)
    vmem = pl.BlockSpec(memory_space=pltpu.VMEM)
    limit = 60 * 1024 * 1024
    operands = (
        innovation,
        cluster,
        kernel.reshape(levels * width, lanes),
        wind_x.reshape(levels * width, lanes),
        wind_y.reshape(levels * width, lanes),
        conv_strength,
        conv_matrix,
    )
    field_shape = jax.ShapeDtypeStruct((adjoints * levels * width, lanes), jnp.float32)
    table_shape = jax.ShapeDtypeStruct((nx * ny, adjoints * width, lanes), jnp.float32)
    field, surfaces = pl.pallas_call(
        functools.partial(kernel_body, (levels, width, adjoints, n_t, n_s)),
        out_shape=(field_shape, table_shape),
        in_specs=[anywhere] * len(operands),
        out_specs=(anywhere, anywhere),
        scratch_shapes=[pltpu.VMEM(x.shape, x.dtype) for x in operands]
        + [
            pltpu.VMEM((width + 4, padded, lanes), jnp.float32),
            pltpu.VMEM((width + 3, padded, lanes), jnp.float32),
            pltpu.VMEM((width + 2, padded, lanes), jnp.float32),
            pltpu.VMEM((nx * ny, padded, lanes), jnp.float32),
            pltpu.VMEM((ny, padded, lanes), jnp.float32),
            pltpu.VMEM((width + 2, adjoints, padded, lanes), jnp.float32),
            pltpu.VMEM(table_shape.shape, jnp.float32),
            pltpu.VMEM(field_shape.shape, jnp.float32),
            pltpu.VMEM((depth, depth), jnp.float32),
            pltpu.SemaphoreType.DMA((n_sems,)),
            pltpu.SemaphoreType.DMA((n_sems,)),
            pltpu.SemaphoreType.DMA((len(operands),)),
            pltpu.SemaphoreType.DMA((adjoints * padded // 8 + 1,)),
        ],
        compiler_params=pltpu.CompilerParams(
            collective_id=0, has_side_effects=True, vmem_limit_bytes=limit
        ),
    )(*operands)
    field, sensed = pl.pallas_call(
        functools.partial(gather_body, (width, adjoints, n_t, n_s)),
        out_shape=(field_shape, jax.ShapeDtypeStruct((adjoints, elements), jnp.float32)),
        in_specs=[vmem, vmem, anywhere, anywhere],
        out_specs=(anywhere, vmem),
        scratch_shapes=[
            pltpu.VMEM(table_shape.shape, jnp.float32),
            pltpu.SemaphoreType.DMA((adjoints,)),
            pltpu.SemaphoreType.DMA,
        ],
        compiler_params=pltpu.CompilerParams(vmem_limit_bytes=limit),
    )(margin_cell.T, margin_weight.T, surfaces, field)
    return field.reshape(adjoints, levels, width, lanes), sensed


def solution(mesh):
    in_specs = (
        P(("groups", "tiles"), "sub"),
        P(("groups", "tiles"), "sub"),
        P(None, "tiles", "sub"),
        P(None, "tiles", "sub"),
        P(None, "tiles", "sub"),
        P("tiles", "sub"),
        P(),
        P(("tiles", "sub"), None),
        P(("tiles", "sub"), None),
    )
    out_specs = (P(("groups", "adj"), None, "tiles", "sub"), P(("groups", "adj"), ("tiles", "sub")))
    return jax.shard_map(body, mesh=mesh, in_specs=in_specs, out_specs=out_specs, check_vma=False)
```

```python
import functools

import jax
import jax.numpy as jnp
from jax import lax
from jax.experimental import pallas as pl
from jax.experimental.pallas import tpu as pltpu
from jax.sharding import PartitionSpec as P

ADJ = 8
NSTEP = 2
MESH = pl.DeviceIdType.MESH


def offsets(count):
    return [0, 1, -1][: min(3, count)]


def slot_of(offset, count):
    return offset % min(3, count)


def divmod_const(value, number):
    if number & (number - 1) == 0:
        return value >> (number.bit_length() - 1), value & (number - 1)
    return value // number, value % number


def split(value):
    high = value.astype(jnp.bfloat16).astype(jnp.float32)
    return high, value - high


def stacked(value, depth):
    high, low = split(value)
    rows, lanes = value.shape
    parts = [high, low, high]
    if depth > 3 * rows:
        parts.append(jnp.zeros((depth - 3 * rows, lanes), jnp.float32))
    return jnp.concatenate(parts, axis=0).astype(jnp.bfloat16)


def kernel_body(
    dims,
    *refs,
):
    sources, (field, surfaces), scratch = refs[:7], refs[7:9], refs[9:]
    arrivals, scratch = scratch[:7], scratch[7:]
    innovation, cluster, kernel, wind_x, wind_y, strength, matrix = arrivals
    (
        base,
        face_x,
        face_y,
        pack_a,
        pack_b,
        state,
        table,
        held,
        square,
        send_sem,
        recv_sem,
        load_sem,
        store_sem,
    ) = scratch
    levels, width, adjoints, n_t, n_s = dims
    padded = base.shape[1]
    lanes = base.shape[2]
    depth = square.shape[0]
    me_g = lax.axis_index("groups")
    me_t = lax.axis_index("tiles")
    me_s = lax.axis_index("sub")
    me_a = lax.axis_index("adj")
    nx, ny = min(3, n_t), min(3, n_s)

    def device(dt, ds):
        return (me_g, lax.rem(me_t + dt + n_t, n_t), lax.rem(me_s + ds + n_s, n_s), me_a)

    partners = [(dt, ds) for dt in offsets(n_t) for ds in offsets(n_s) if (dt, ds) != (0, 0)]
    barrier = pltpu.get_barrier_semaphore()
    for dt, ds in partners:
        pl.semaphore_signal(barrier, inc=1, device_id=device(dt, ds), device_id_type=MESH)
    loads = [
        pltpu.make_async_copy(source, arrival, load_sem.at[i])
        for i, (source, arrival) in enumerate(zip(sources, arrivals))
    ]
    for i in (6, 2, 0, 1, 5, 3, 4):
        loads[i].start()

    count = [0]

    def send(src, dst, dt, ds):
        at = count[0]
        count[0] += 1
        copy = pltpu.make_async_remote_copy(
            src_ref=src,
            dst_ref=dst,
            send_sem=send_sem.at[at],
            recv_sem=recv_sem.at[at],
            device_id=device(dt, ds),
            device_id_type=MESH,
        )
        copy.start()
        return copy

    square[...] = jnp.zeros_like(square)
    loads[6].wait()
    square[0:levels, 0:levels] = matrix[...]
    high, low = split(square[...].T)
    mixer = high + pltpu.roll(high, padded, 1) + pltpu.roll(low, 2 * padded, 1)
    mixer = mixer[0:padded].astype(jnp.bfloat16)

    def mix(value):
        return jnp.dot(mixer, stacked(value, depth), preferred_element_type=jnp.float32)

    lane = lax.broadcasted_iota(jnp.int32, (padded, lanes), 1)
    pair = ((lane + 1) & (lanes - 1)) >> 1
    level = lax.broadcasted_iota(jnp.int32, (padded, lanes), 0)

    last = levels // 8 * 8
    for load in loads[:6]:
        load.wait()

    def prepare(x, packed):
        rows = pl.ds(x, levels, stride=width)
        empty = jnp.zeros((padded - last, lanes), jnp.float32)
        face_x[2 + x, last:padded, :] = empty
        face_y[1 + x, last:padded, :] = empty
        base[2 + x, last:padded, :] = empty
        face_x[2 + x, 0:levels, :] = wind_x[rows, :]
        face_y[1 + x, 0:levels, :] = wind_y[rows, :]
        base[2 + x, 0:levels, :] = kernel[rows, :]
        column = base[2 + x]
        one = pl.ds(x, 1)
        mixed = mix(column)
        column = (column + strength[one, :] * (mixed - column)) * innovation[one, :]
        column = jnp.where(level == levels, cluster[one, :].astype(jnp.float32), column)
        column = jnp.where(level == levels + 1, strength[one, :], column)
        base[2 + x] = column
        packed = jnp.where(pair == x, pltpu.roll(column, 2 * x, 1), packed)
        faces = face_y[1 + x]
        packed = jnp.where(pair == width + x, pltpu.roll(faces, 2 * (width + x), 1), packed)
        return packed

    packed = jnp.zeros((padded, lanes), jnp.float32)
    for x in (0, 1, width - 2, width - 1):
        packed = prepare(x, packed)
    pl.semaphore_wait(barrier, len(partners))
    copies_x = [
        send(base.at[pl.ds(width, 2)], base.at[pl.ds(0, 2)], 1, 0),
        send(base.at[pl.ds(2, 2)], base.at[pl.ds(width + 2, 2)], -1, 0),
        send(face_x.at[pl.ds(width, 2)], face_x.at[pl.ds(0, 2)], 1, 0),
        send(face_x.at[2], face_x.at[width + 2], -1, 0),
        send(face_y.at[width], face_y.at[0], 1, 0),
        send(face_y.at[1], face_y.at[width + 1], -1, 0),
    ]
    packed = lax.fori_loop(2, width - 2, prepare, packed, unroll=True)
    pack_a[0] = packed
    near, far = [], []
    for dt, ds in partners:
        if ds != 0:
            there = slot_of(-dt, n_t) * ny + slot_of(-ds, n_s)
            copy = send(pack_a.at[0], pack_a.at[there], dt, ds)
            (far if dt else near).append(copy)
    for copy in near:
        copy.wait()

    odd = (lane & 1) == 1
    has_south = jnp.where(me_s > 0, 1.0, 0.0)
    has_north = jnp.where(me_s < n_s - 1, 1.0, 0.0)

    def merged(pack, dt):
        row = slot_of(dt, n_t) * ny
        south = pltpu.roll(pack[row + slot_of(-1, n_s)], 2, 1) * has_south
        north = pack[row + slot_of(1, n_s)] * has_north
        return jnp.where(odd, south, north)

    def edges(pack, at, value):
        seam = pltpu.roll(pack, lanes - 1 - 2 * at, 1)
        rows = lane[0 : value.shape[0]]
        north = jnp.where(rows == lanes - 1, seam, pltpu.roll(value, lanes - 1, 1))
        south = jnp.where(rows == 0, seam, pltpu.roll(value, 1, 1))
        return north, south

    seam_a = merged(pack_a, 0)
    first_id = (me_a * adjoints).astype(jnp.float32)

    def advance(x, seam, at):
        flow_y = face_y[1 + x]
        _, flow_south = edges(seam, width + at, flow_y)
        east_rate = jnp.maximum(face_x[2 + x], 0.0)
        west_rate = jnp.minimum(face_x[1 + x], 0.0)
        north_rate = jnp.maximum(flow_y, 0.0)
        south_rate = jnp.minimum(flow_south, 0.0)
        center_rate = 1.0 - east_rate + west_rate - north_rate + south_rate
        center, east, west = base[2 + x], base[3 + x], base[1 + x]
        north, south = edges(seam, at, center)
        terms = [
            (center * center_rate, center),
            (east * east_rate, east),
            (-west * west_rate, west),
            (north * north_rate, north),
            (-south * south_rate, south),
        ]
        values = []
        for a in range(adjoints):
            total = None
            for product, source in terms:
                ids = source[levels : levels + 1, :]
                chosen = jnp.where(ids == first_id + a, 1.0, 0.0)
                part = product * chosen
                total = part if total is None else total + part
            values.append(total)
        mixed = mix(jnp.concatenate(values, axis=1))
        fraction = center[levels + 1 : levels + 2, :]
        results = []
        for a in range(adjoints):
            value = values[a]
            value = value + fraction * (mixed[:, a * lanes : (a + 1) * lanes] - value)
            state[1 + x, a] = value
            results.append(value)
        return results

    def inside(x, packed):
        for a, value in enumerate(advance(x, seam_a, x)):
            at = a * width + x
            packed = jnp.where(pair == at, pltpu.roll(value, 2 * at, 1), packed)
        return packed

    packed = jnp.zeros((padded, lanes), jnp.float32)
    packed = lax.fori_loop(1, width - 1, inside, packed, unroll=True)
    for copy in copies_x:
        copy.wait()
    packed = inside(0, packed)
    packed = inside(width - 1, packed)
    pack_b[0] = packed
    copies = [
        send(pack_b.at[0], pack_b.at[slot_of(-ds, n_s)], 0, ds) for ds in offsets(n_s) if ds != 0
    ]
    for copy in far:
        copy.wait()
    advance(-1, merged(pack_a, -1), width - 1)
    advance(width, merged(pack_a, 1), 0)
    for copy in copies:
        copy.wait()
    seam_b = merged(pack_b, 0)

    stores = []

    def transport(low, high):
        top = min(high, levels)

        def along(x, carry):
            flow_y = face_y[1 + x, low:high]
            _, flow_south = edges(seam_a[low:high], width + x, flow_y)
            east_rate = jnp.maximum(face_x[2 + x, low:high], 0.0)
            west_rate = jnp.minimum(face_x[1 + x, low:high], 0.0)
            north_rate = jnp.maximum(flow_y, 0.0)
            south_rate = jnp.minimum(flow_south, 0.0)
            center_rate = 1.0 - east_rate + west_rate - north_rate + south_rate
            for a in range(adjoints):
                center = state[1 + x, a, low:high]
                north, south = edges(seam_b[low:high], a * width + x, center)
                value = (
                    center * center_rate
                    + east_rate * state[2 + x, a, low:high]
                    - west_rate * state[x, a, low:high]
                    + north_rate * north
                    - south_rate * south
                )
                rows = pl.ds((a * levels + low) * width + x, top - low, stride=width)
                held[rows, :] = value[0 : top - low, :]
                if low == 0:
                    table[0, pl.ds(a * width + x, 1), :] = value[0:1, :]
            return carry

        lax.fori_loop(0, width, along, 0, unroll=True)

    def store(low, high):
        top = min(high, levels)
        for a in range(adjoints):
            rows = pl.ds((a * levels + low) * width, (top - low) * width)
            copy = pltpu.make_async_copy(held.at[rows], field.at[rows], store_sem.at[len(stores)])
            copy.start()
            stores.append(copy)

    transport(0, 8)
    copies = []
    for dt, ds in partners:
        there = slot_of(-dt, n_t) * ny + slot_of(-ds, n_s)
        copies.append(send(table.at[0], table.at[there], dt, ds))
    store(0, 8)
    for low in range(8, padded, 8):
        transport(low, low + 8)
        store(low, low + 8)
    for copy in copies:
        copy.wait()
    own = pltpu.make_async_copy(table, surfaces, store_sem.at[len(stores)])
    own.start()
    for copy in stores:
        copy.wait()
    own.wait()


def gather_body(dims, cells, weights, surfaces, field, field_out, sensed, table, held, load_sem, store_sem, table_sem):
    width, adjoints, n_t, n_s = dims
    lanes = table.shape[2]
    nx, ny = min(3, n_t), min(3, n_s)
    me_t = lax.axis_index("tiles")
    me_s = lax.axis_index("sub")
    arrival = pltpu.make_async_copy(surfaces, table, table_sem)
    arrival.start()
    share = field.shape[0] // adjoints
    loads, stores = [], []
    for a in range(adjoints):
        rows = pl.ds(a * share, share)
        loads.append(pltpu.make_async_copy(field.at[rows], held.at[rows], load_sem.at[a]))
        stores.append(pltpu.make_async_copy(held.at[rows], field_out.at[rows], store_sem.at[a]))
        loads[a].start()

    column, row = divmod_const(cells[...], n_s * lanes)
    tile, in_tile = divmod_const(column, width)
    block, in_block = divmod_const(row, lanes)
    step_t = tile - me_t
    step_t = jnp.where(step_t < 0, step_t + n_t, step_t)
    step_t = jnp.where(step_t > 1, 2, step_t)
    step_s = block - me_s
    step_s = jnp.where(step_s < 0, step_s + ny, step_s)
    table_row = (step_t * ny + step_s) * width + in_tile
    elements = cells.shape[1]
    chunks = elements // lanes
    slots = cells.shape[0]

    arrival.wait()

    def pick(at, carry):
        slot, x = divmod_const(at, width)
        taken = list(carry)
        masks = [table_row[:, c * lanes : (c + 1) * lanes] == at for c in range(chunks)]
        for a in range(adjoints):
            line = jnp.broadcast_to(table[slot, pl.ds(a * width + x, 1), :], (slots, lanes))
            for c in range(chunks):
                found = jnp.take_along_axis(
                    line, in_block[:, c * lanes : (c + 1) * lanes], axis=1, mode="promise_in_bounds"
                )
                i = a * chunks + c
                taken[i] = jnp.where(masks[c], found, taken[i])
        return tuple(taken)

    empty = jnp.zeros((slots, lanes), jnp.float32)
    taken = lax.fori_loop(0, width, pick, (empty,) * (adjoints * chunks), unroll=4)
    for load, store in zip(loads, stores):
        load.wait()
        store.start()
    taken = lax.fori_loop(width, nx * ny * width, pick, taken, unroll=4)
    for a in range(adjoints):
        for c in range(chunks):
            part = taken[a * chunks + c] * weights[:, c * lanes : (c + 1) * lanes]
            sensed[a : a + 1, c * lanes : (c + 1) * lanes] = jnp.sum(part, axis=0, keepdims=True)
    for store in stores:
        store.wait()


def body(
    innovation,
    cluster,
    kernel,
    wind_x,
    wind_y,
    conv_strength,
    conv_matrix,
    margin_cell,
    margin_weight,
):
    levels, width, lanes = kernel.shape
    n_t, n_s = lax.axis_size("tiles"), lax.axis_size("sub")
    adjoints = ADJ // lax.axis_size("adj")
    elements, slots = margin_cell.shape
    padded = 8 * pl.cdiv(levels + 2, 8)
    depth = 128 * pl.cdiv(3 * padded, 128)
    nx, ny = min(3, n_t), min(3, n_s)
    n_sems = 6 + 2 * (nx * ny - 1) - (nx - 1) + ny - 1
    anywhere = pl.BlockSpec(memory_space=pl.ANY)
    vmem = pl.BlockSpec(memory_space=pltpu.VMEM)
    limit = 60 * 1024 * 1024
    operands = (
        innovation,
        cluster,
        kernel.reshape(levels * width, lanes),
        wind_x.reshape(levels * width, lanes),
        wind_y.reshape(levels * width, lanes),
        conv_strength,
        conv_matrix,
    )
    field_shape = jax.ShapeDtypeStruct((adjoints * levels * width, lanes), jnp.float32)
    table_shape = jax.ShapeDtypeStruct((nx * ny, adjoints * width, lanes), jnp.float32)
    field, surfaces = pl.pallas_call(
        functools.partial(kernel_body, (levels, width, adjoints, n_t, n_s)),
        out_shape=(field_shape, table_shape),
        in_specs=[anywhere] * len(operands),
        out_specs=(anywhere, anywhere),
        scratch_shapes=[pltpu.VMEM(x.shape, x.dtype) for x in operands]
        + [
            pltpu.VMEM((width + 4, padded, lanes), jnp.float32),
            pltpu.VMEM((width + 3, padded, lanes), jnp.float32),
            pltpu.VMEM((width + 2, padded, lanes), jnp.float32),
            pltpu.VMEM((nx * ny, padded, lanes), jnp.float32),
            pltpu.VMEM((ny, padded, lanes), jnp.float32),
            pltpu.VMEM((width + 2, adjoints, padded, lanes), jnp.float32),
            pltpu.VMEM(table_shape.shape, jnp.float32),
            pltpu.VMEM(field_shape.shape, jnp.float32),
            pltpu.VMEM((depth, depth), jnp.float32),
            pltpu.SemaphoreType.DMA((n_sems,)),
            pltpu.SemaphoreType.DMA((n_sems,)),
            pltpu.SemaphoreType.DMA((len(operands),)),
            pltpu.SemaphoreType.DMA((adjoints * padded // 8 + 1,)),
        ],
        compiler_params=pltpu.CompilerParams(
            collective_id=0, has_side_effects=True, vmem_limit_bytes=limit
        ),
    )(*operands)
    field, sensed = pl.pallas_call(
        functools.partial(gather_body, (width, adjoints, n_t, n_s)),
        out_shape=(field_shape, jax.ShapeDtypeStruct((adjoints, elements), jnp.float32)),
        in_specs=[vmem, vmem, anywhere, anywhere],
        out_specs=(anywhere, vmem),
        scratch_shapes=[
            pltpu.VMEM(table_shape.shape, jnp.float32),
            pltpu.VMEM(field_shape.shape, jnp.float32),
            pltpu.SemaphoreType.DMA((adjoints,)),
            pltpu.SemaphoreType.DMA((adjoints,)),
            pltpu.SemaphoreType.DMA,
        ],
        compiler_params=pltpu.CompilerParams(vmem_limit_bytes=limit),
    )(margin_cell.T, margin_weight.T, surfaces, field)
    return field.reshape(adjoints, levels, width, lanes), sensed


def solution(mesh):
    in_specs = (
        P(("groups", "tiles"), "sub"),
        P(("groups", "tiles"), "sub"),
        P(None, "tiles", "sub"),
        P(None, "tiles", "sub"),
        P(None, "tiles", "sub"),
        P("tiles", "sub"),
        P(),
        P(("tiles", "sub"), None),
        P(("tiles", "sub"), None),
    )
    out_specs = (P(("groups", "adj"), None, "tiles", "sub"), P(("groups", "adj"), ("tiles", "sub")))
    return jax.shard_map(body, mesh=mesh, in_specs=in_specs, out_specs=out_specs, check_vma=False)
```

```python
import functools

import jax
import jax.numpy as jnp
from jax import lax
from jax.experimental import pallas as pl
from jax.experimental.pallas import tpu as pltpu
from jax.sharding import PartitionSpec as P

ADJ = 8
NSTEP = 2
MESH = pl.DeviceIdType.MESH


def offsets(count):
    return [0, 1, -1][: min(3, count)]


def slot_of(offset, count):
    return offset % min(3, count)


def divmod_const(value, number):
    if number & (number - 1) == 0:
        return value >> (number.bit_length() - 1), value & (number - 1)
    return value // number, value % number


def split(value):
    high = value.astype(jnp.bfloat16).astype(jnp.float32)
    return high, value - high


def stacked(value, depth):
    high, low = split(value)
    rows, lanes = value.shape
    parts = [high, low, high]
    if depth > 3 * rows:
        parts.append(jnp.zeros((depth - 3 * rows, lanes), jnp.float32))
    return jnp.concatenate(parts, axis=0).astype(jnp.bfloat16)


def kernel_body(
    dims,
    *refs,
):
    sources, (field, surfaces), scratch = refs[:7], refs[7:9], refs[9:]
    arrivals, scratch = scratch[:7], scratch[7:]
    innovation, cluster, kernel, wind_x, wind_y, strength, matrix = arrivals
    (
        base,
        face_x,
        face_y,
        pack_a,
        pack_b,
        state,
        table,
        held,
        square,
        send_sem,
        recv_sem,
        load_sem,
        store_sem,
    ) = scratch
    levels, width, adjoints, n_t, n_s = dims
    padded = base.shape[1]
    lanes = base.shape[2]
    depth = square.shape[0]
    me_g = lax.axis_index("groups")
    me_t = lax.axis_index("tiles")
    me_s = lax.axis_index("sub")
    me_a = lax.axis_index("adj")
    nx, ny = min(3, n_t), min(3, n_s)

    def device(dt, ds):
        return (me_g, lax.rem(me_t + dt + n_t, n_t), lax.rem(me_s + ds + n_s, n_s), me_a)

    partners = [(dt, ds) for dt in offsets(n_t) for ds in offsets(n_s) if (dt, ds) != (0, 0)]
    barrier = pltpu.get_barrier_semaphore()
    for dt, ds in partners:
        pl.semaphore_signal(barrier, inc=1, device_id=device(dt, ds), device_id_type=MESH)
    loads = [
        pltpu.make_async_copy(source, arrival, load_sem.at[i])
        for i, (source, arrival) in enumerate(zip(sources, arrivals))
    ]
    for i in (6, 2, 0, 1, 5, 3, 4):
        loads[i].start()

    count = [0]

    def send(src, dst, dt, ds):
        at = count[0]
        count[0] += 1
        copy = pltpu.make_async_remote_copy(
            src_ref=src,
            dst_ref=dst,
            send_sem=send_sem.at[at],
            recv_sem=recv_sem.at[at],
            device_id=device(dt, ds),
            device_id_type=MESH,
        )
        copy.start()
        return copy

    square[...] = jnp.zeros_like(square)
    loads[6].wait()
    square[0:levels, 0:levels] = matrix[...]
    high, low = split(square[...].T)
    mixer = high + pltpu.roll(high, padded, 1) + pltpu.roll(low, 2 * padded, 1)
    mixer = mixer[0:padded].astype(jnp.bfloat16)

    def mix(value):
        return jnp.dot(mixer, stacked(value, depth), preferred_element_type=jnp.float32)

    lane = lax.broadcasted_iota(jnp.int32, (padded, lanes), 1)
    pair = ((lane + 1) & (lanes - 1)) >> 1
    level = lax.broadcasted_iota(jnp.int32, (padded, lanes), 0)

    last = levels // 8 * 8
    for load in loads[:6]:
        load.wait()

    def prepare(x, packed):
        rows = pl.ds(x, levels, stride=width)
        empty = jnp.zeros((padded - last, lanes), jnp.float32)
        face_x[2 + x, last:padded, :] = empty
        face_y[1 + x, last:padded, :] = empty
        base[2 + x, last:padded, :] = empty
        face_x[2 + x, 0:levels, :] = wind_x[rows, :]
        face_y[1 + x, 0:levels, :] = wind_y[rows, :]
        base[2 + x, 0:levels, :] = kernel[rows, :]
        column = base[2 + x]
        one = pl.ds(x, 1)
        mixed = mix(column)
        column = (column + strength[one, :] * (mixed - column)) * innovation[one, :]
        column = jnp.where(level == levels, cluster[one, :].astype(jnp.float32), column)
        column = jnp.where(level == levels + 1, strength[one, :], column)
        base[2 + x] = column
        packed = jnp.where(pair == x, pltpu.roll(column, 2 * x, 1), packed)
        faces = face_y[1 + x]
        packed = jnp.where(pair == width + x, pltpu.roll(faces, 2 * (width + x), 1), packed)
        return packed

    packed = jnp.zeros((padded, lanes), jnp.float32)
    for x in (0, 1, width - 2, width - 1):
        packed = prepare(x, packed)
    pl.semaphore_wait(barrier, len(partners))
    copies_x = [
        send(base.at[pl.ds(width, 2)], base.at[pl.ds(0, 2)], 1, 0),
        send(base.at[pl.ds(2, 2)], base.at[pl.ds(width + 2, 2)], -1, 0),
        send(face_x.at[pl.ds(width, 2)], face_x.at[pl.ds(0, 2)], 1, 0),
        send(face_x.at[2], face_x.at[width + 2], -1, 0),
        send(face_y.at[width], face_y.at[0], 1, 0),
        send(face_y.at[1], face_y.at[width + 1], -1, 0),
    ]
    packed = lax.fori_loop(2, width - 2, prepare, packed, unroll=True)
    pack_a[0] = packed
    near, far = [], []
    for dt, ds in partners:
        if ds != 0:
            there = slot_of(-dt, n_t) * ny + slot_of(-ds, n_s)
            copy = send(pack_a.at[0], pack_a.at[there], dt, ds)
            (far if dt else near).append(copy)
    for copy in near:
        copy.wait()

    odd = (lane & 1) == 1
    has_south = jnp.where(me_s > 0, 1.0, 0.0)
    has_north = jnp.where(me_s < n_s - 1, 1.0, 0.0)

    def merged(pack, dt):
        row = slot_of(dt, n_t) * ny
        south = pltpu.roll(pack[row + slot_of(-1, n_s)], 2, 1) * has_south
        north = pack[row + slot_of(1, n_s)] * has_north
        return jnp.where(odd, south, north)

    def edges(pack, at, value):
        seam = pltpu.roll(pack, lanes - 1 - 2 * at, 1)
        rows = lane[0 : value.shape[0]]
        north = jnp.where(rows == lanes - 1, seam, pltpu.roll(value, lanes - 1, 1))
        south = jnp.where(rows == 0, seam, pltpu.roll(value, 1, 1))
        return north, south

    seam_a = merged(pack_a, 0)
    first_id = (me_a * adjoints).astype(jnp.float32)

    def advance(x, seam, at):
        flow_y = face_y[1 + x]
        _, flow_south = edges(seam, width + at, flow_y)
        east_rate = jnp.maximum(face_x[2 + x], 0.0)
        west_rate = jnp.minimum(face_x[1 + x], 0.0)
        north_rate = jnp.maximum(flow_y, 0.0)
        south_rate = jnp.minimum(flow_south, 0.0)
        center_rate = 1.0 - east_rate + west_rate - north_rate + south_rate
        center, east, west = base[2 + x], base[3 + x], base[1 + x]
        north, south = edges(seam, at, center)
        terms = [
            (center * center_rate, center),
            (east * east_rate, east),
            (-west * west_rate, west),
            (north * north_rate, north),
            (-south * south_rate, south),
        ]
        values = []
        for a in range(adjoints):
            total = None
            for product, source in terms:
                ids = source[levels : levels + 1, :]
                chosen = jnp.where(ids == first_id + a, 1.0, 0.0)
                part = product * chosen
                total = part if total is None else total + part
            values.append(total)
        mixed = mix(jnp.concatenate(values, axis=1))
        fraction = center[levels + 1 : levels + 2, :]
        results = []
        for a in range(adjoints):
            value = values[a]
            value = value + fraction * (mixed[:, a * lanes : (a + 1) * lanes] - value)
            state[1 + x, a] = value
            results.append(value)
        return results

    def inside(x, packed):
        for a, value in enumerate(advance(x, seam_a, x)):
            at = a * width + x
            packed = jnp.where(pair == at, pltpu.roll(value, 2 * at, 1), packed)
        return packed

    packed = jnp.zeros((padded, lanes), jnp.float32)
    packed = lax.fori_loop(1, width - 1, inside, packed, unroll=True)
    for copy in copies_x:
        copy.wait()
    packed = inside(0, packed)
    packed = inside(width - 1, packed)
    pack_b[0] = packed
    copies = [
        send(pack_b.at[0], pack_b.at[slot_of(-ds, n_s)], 0, ds) for ds in offsets(n_s) if ds != 0
    ]
    for copy in far:
        copy.wait()
    advance(-1, merged(pack_a, -1), width - 1)
    advance(width, merged(pack_a, 1), 0)
    for copy in copies:
        copy.wait()
    seam_b = merged(pack_b, 0)

    stores = []

    def transport(low, high):
        top = min(high, levels)

        def along(x, carry):
            flow_y = face_y[1 + x, low:high]
            _, flow_south = edges(seam_a[low:high], width + x, flow_y)
            east_rate = jnp.maximum(face_x[2 + x, low:high], 0.0)
            west_rate = jnp.minimum(face_x[1 + x, low:high], 0.0)
            north_rate = jnp.maximum(flow_y, 0.0)
            south_rate = jnp.minimum(flow_south, 0.0)
            center_rate = 1.0 - east_rate + west_rate - north_rate + south_rate
            for a in range(adjoints):
                center = state[1 + x, a, low:high]
                north, south = edges(seam_b[low:high], a * width + x, center)
                value = (
                    center * center_rate
                    + east_rate * state[2 + x, a, low:high]
                    - west_rate * state[x, a, low:high]
                    + north_rate * north
                    - south_rate * south
                )
                rows = pl.ds((a * levels + low) * width + x, top - low, stride=width)
                held[rows, :] = value[0 : top - low, :]
                if low == 0:
                    table[0, pl.ds(a * width + x, 1), :] = value[0:1, :]
            return carry

        lax.fori_loop(0, width, along, 0, unroll=True)

    def store(low, high):
        top = min(high, levels)
        for a in range(adjoints):
            rows = pl.ds((a * levels + low) * width, (top - low) * width)
            copy = pltpu.make_async_copy(held.at[rows], field.at[rows], store_sem.at[len(stores)])
            copy.start()
            stores.append(copy)

    transport(0, 8)
    copies = []
    for dt, ds in partners:
        there = slot_of(-dt, n_t) * ny + slot_of(-ds, n_s)
        copies.append(send(table.at[0], table.at[there], dt, ds))
    store(0, 8)
    for low in range(8, padded, 8):
        transport(low, low + 8)
        store(low, low + 8)
    for copy in copies:
        copy.wait()
    own = pltpu.make_async_copy(table, surfaces, store_sem.at[len(stores)])
    own.start()
    for copy in stores:
        copy.wait()
    own.wait()


def gather_body(dims, cells, weights, surfaces, field, field_out, sensed, table, held, load_sem, store_sem, table_sem):
    width, adjoints, n_t, n_s = dims
    lanes = table.shape[2]
    nx, ny = min(3, n_t), min(3, n_s)
    me_t = lax.axis_index("tiles")
    me_s = lax.axis_index("sub")
    arrival = pltpu.make_async_copy(surfaces, table, table_sem)
    arrival.start()
    share = field.shape[0] // adjoints
    loads, stores = [], []
    for a in range(adjoints):
        rows = pl.ds(a * share, share)
        loads.append(pltpu.make_async_copy(field.at[rows], held.at[rows], load_sem.at[a]))
        stores.append(pltpu.make_async_copy(held.at[rows], field_out.at[rows], store_sem.at[a]))
        loads[a].start()

    column, row = divmod_const(cells[...], n_s * lanes)
    tile, in_tile = divmod_const(column, width)
    block, in_block = divmod_const(row, lanes)
    step_t = tile - me_t
    step_t = jnp.where(step_t < 0, step_t + n_t, step_t)
    step_t = jnp.where(step_t > 1, 2, step_t)
    step_s = block - me_s
    step_s = jnp.where(step_s < 0, step_s + ny, step_s)
    table_row = (step_t * ny + step_s) * width + in_tile
    elements = cells.shape[1]
    slots = cells.shape[0]
    chunk = 2 * lanes if elements % (2 * lanes) == 0 else lanes
    lane_of = lax.broadcasted_iota(jnp.int32, (lanes, chunk), 0)
    row_of = lax.broadcasted_iota(jnp.int32, (nx * ny * width, chunk), 0)

    arrival.wait()
    surface = table[...].reshape(nx * ny * adjoints * width, lanes)
    high, low = split(surface)
    surface = jnp.concatenate([high, low], axis=1).astype(jnp.bfloat16)

    for c in range(elements // chunk):
        span = slice(c * chunk, (c + 1) * chunk)
        totals = [jnp.zeros((8, chunk), jnp.float32)] * adjoints
        for k in range(slots):
            chosen = jnp.where(lane_of == in_block[k : k + 1, span], 1.0, 0.0).astype(jnp.bfloat16)
            chosen = jnp.concatenate([chosen, chosen], axis=0)
            lines = jnp.dot(surface, chosen, preferred_element_type=jnp.float32)
            share_of = jnp.where(row_of == table_row[k : k + 1, span], weights[k : k + 1, span], 0.0)
            for a in range(adjoints):
                for block in range(nx * ny):
                    for x in range(0, width, 8):
                        line = (block * adjoints + a) * width + x
                        mine = block * width + x
                        totals[a] += lines[line : line + 8] * share_of[mine : mine + 8]
        for a in range(adjoints):
            sensed[a : a + 1, span] = jnp.sum(totals[a], axis=0, keepdims=True)
        if c == 0:
            for load, store in zip(loads, stores):
                load.wait()
                store.start()
    for store in stores:
        store.wait()


def body(
    innovation,
    cluster,
    kernel,
    wind_x,
    wind_y,
    conv_strength,
    conv_matrix,
    margin_cell,
    margin_weight,
):
    levels, width, lanes = kernel.shape
    n_t, n_s = lax.axis_size("tiles"), lax.axis_size("sub")
    adjoints = ADJ // lax.axis_size("adj")
    elements, slots = margin_cell.shape
    padded = 8 * pl.cdiv(levels + 2, 8)
    depth = 128 * pl.cdiv(3 * padded, 128)
    nx, ny = min(3, n_t), min(3, n_s)
    n_sems = 6 + 2 * (nx * ny - 1) - (nx - 1) + ny - 1
    anywhere = pl.BlockSpec(memory_space=pl.ANY)
    vmem = pl.BlockSpec(memory_space=pltpu.VMEM)
    limit = 60 * 1024 * 1024
    operands = (
        innovation,
        cluster,
        kernel.reshape(levels * width, lanes),
        wind_x.reshape(levels * width, lanes),
        wind_y.reshape(levels * width, lanes),
        conv_strength,
        conv_matrix,
    )
    field_shape = jax.ShapeDtypeStruct((adjoints * levels * width, lanes), jnp.float32)
    table_shape = jax.ShapeDtypeStruct((nx * ny, adjoints * width, lanes), jnp.float32)
    field, surfaces = pl.pallas_call(
        functools.partial(kernel_body, (levels, width, adjoints, n_t, n_s)),
        out_shape=(field_shape, table_shape),
        in_specs=[anywhere] * len(operands),
        out_specs=(anywhere, anywhere),
        scratch_shapes=[pltpu.VMEM(x.shape, x.dtype) for x in operands]
        + [
            pltpu.VMEM((width + 4, padded, lanes), jnp.float32),
            pltpu.VMEM((width + 3, padded, lanes), jnp.float32),
            pltpu.VMEM((width + 2, padded, lanes), jnp.float32),
            pltpu.VMEM((nx * ny, padded, lanes), jnp.float32),
            pltpu.VMEM((ny, padded, lanes), jnp.float32),
            pltpu.VMEM((width + 2, adjoints, padded, lanes), jnp.float32),
            pltpu.VMEM(table_shape.shape, jnp.float32),
            pltpu.VMEM(field_shape.shape, jnp.float32),
            pltpu.VMEM((depth, depth), jnp.float32),
            pltpu.SemaphoreType.DMA((n_sems,)),
            pltpu.SemaphoreType.DMA((n_sems,)),
            pltpu.SemaphoreType.DMA((len(operands),)),
            pltpu.SemaphoreType.DMA((adjoints * padded // 8 + 1,)),
        ],
        compiler_params=pltpu.CompilerParams(
            collective_id=0, has_side_effects=True, vmem_limit_bytes=limit
        ),
    )(*operands)
    field, sensed = pl.pallas_call(
        functools.partial(gather_body, (width, adjoints, n_t, n_s)),
        out_shape=(field_shape, jax.ShapeDtypeStruct((adjoints, elements), jnp.float32)),
        in_specs=[vmem, vmem, anywhere, anywhere],
        out_specs=(anywhere, vmem),
        scratch_shapes=[
            pltpu.VMEM(table_shape.shape, jnp.float32),
            pltpu.VMEM(field_shape.shape, jnp.float32),
            pltpu.SemaphoreType.DMA((adjoints,)),
            pltpu.SemaphoreType.DMA((adjoints,)),
            pltpu.SemaphoreType.DMA,
        ],
        compiler_params=pltpu.CompilerParams(vmem_limit_bytes=limit),
    )(margin_cell.T, margin_weight.T, surfaces, field)
    return field.reshape(adjoints, levels, width, lanes), sensed


def solution(mesh):
    in_specs = (
        P(("groups", "tiles"), "sub"),
        P(("groups", "tiles"), "sub"),
        P(None, "tiles", "sub"),
        P(None, "tiles", "sub"),
        P(None, "tiles", "sub"),
        P("tiles", "sub"),
        P(),
        P(("tiles", "sub"), None),
        P(("tiles", "sub"), None),
    )
    out_specs = (P(("groups", "adj"), None, "tiles", "sub"), P(("groups", "adj"), ("tiles", "sub")))
    return jax.shard_map(body, mesh=mesh, in_specs=in_specs, out_specs=out_specs, check_vma=False)
```

```python
import functools

import jax
import jax.numpy as jnp
from jax import lax
from jax.experimental import pallas as pl
from jax.experimental.pallas import tpu as pltpu
from jax.sharding import PartitionSpec as P

ADJ = 8
NSTEP = 2
MESH = pl.DeviceIdType.MESH


def offsets(count):
    return [0, 1, -1][: min(3, count)]


def slot_of(offset, count):
    return offset % min(3, count)


def divmod_const(value, number):
    if number & (number - 1) == 0:
        return value >> (number.bit_length() - 1), value & (number - 1)
    return value // number, value % number


def split(value):
    high = value.astype(jnp.bfloat16).astype(jnp.float32)
    return high, value - high


def stacked(value, depth):
    high, low = split(value)
    rows, lanes = value.shape
    parts = [high, low, high]
    if depth > 3 * rows:
        parts.append(jnp.zeros((depth - 3 * rows, lanes), jnp.float32))
    return jnp.concatenate(parts, axis=0).astype(jnp.bfloat16)


def kernel_body(
    dims,
    *refs,
):
    sources, (field, sensed), scratch = refs[:9], refs[9:11], refs[11:]
    arrivals, scratch = scratch[:9], scratch[9:]
    innovation, cluster, kernel, wind_x, wind_y, strength, matrix, cells, weights = arrivals
    (
        base,
        face_x,
        face_y,
        pack_a,
        pack_b,
        state,
        table,
        held,
        square,
        columns,
        shares,
        send_sem,
        recv_sem,
        load_sem,
        store_sem,
    ) = scratch
    levels, width, adjoints, n_t, n_s = dims
    padded = base.shape[1]
    lanes = base.shape[2]
    depth = square.shape[0]
    me_g = lax.axis_index("groups")
    me_t = lax.axis_index("tiles")
    me_s = lax.axis_index("sub")
    me_a = lax.axis_index("adj")
    nx, ny = min(3, n_t), min(3, n_s)

    def device(dt, ds):
        return (me_g, lax.rem(me_t + dt + n_t, n_t), lax.rem(me_s + ds + n_s, n_s), me_a)

    partners = [(dt, ds) for dt in offsets(n_t) for ds in offsets(n_s) if (dt, ds) != (0, 0)]
    barrier = pltpu.get_barrier_semaphore()
    for dt, ds in partners:
        pl.semaphore_signal(barrier, inc=1, device_id=device(dt, ds), device_id_type=MESH)
    loads = [
        pltpu.make_async_copy(source, arrival, load_sem.at[i])
        for i, (source, arrival) in enumerate(zip(sources, arrivals))
    ]
    for i in (6, 2, 0, 1, 5, 3, 4, 7, 8):
        loads[i].start()

    count = [0]

    def send(src, dst, dt, ds):
        at = count[0]
        count[0] += 1
        copy = pltpu.make_async_remote_copy(
            src_ref=src,
            dst_ref=dst,
            send_sem=send_sem.at[at],
            recv_sem=recv_sem.at[at],
            device_id=device(dt, ds),
            device_id_type=MESH,
        )
        copy.start()
        return copy

    square[...] = jnp.zeros_like(square)
    loads[6].wait()
    square[0:levels, 0:levels] = matrix[...]
    high, low = split(square[...].T)
    mixer = high + pltpu.roll(high, padded, 1) + pltpu.roll(low, 2 * padded, 1)
    mixer = mixer[0:padded].astype(jnp.bfloat16)

    def mix(value):
        return jnp.dot(mixer, stacked(value, depth), preferred_element_type=jnp.float32)

    lane = lax.broadcasted_iota(jnp.int32, (padded, lanes), 1)
    pair = ((lane + 1) & (lanes - 1)) >> 1
    level = lax.broadcasted_iota(jnp.int32, (padded, lanes), 0)

    last = levels // 8 * 8
    for load in loads[:6]:
        load.wait()

    def prepare(x, packed):
        rows = pl.ds(x, levels, stride=width)
        empty = jnp.zeros((padded - last, lanes), jnp.float32)
        face_x[2 + x, last:padded, :] = empty
        face_y[1 + x, last:padded, :] = empty
        base[2 + x, last:padded, :] = empty
        face_x[2 + x, 0:levels, :] = wind_x[rows, :]
        face_y[1 + x, 0:levels, :] = wind_y[rows, :]
        base[2 + x, 0:levels, :] = kernel[rows, :]
        column = base[2 + x]
        one = pl.ds(x, 1)
        mixed = mix(column)
        column = (column + strength[one, :] * (mixed - column)) * innovation[one, :]
        column = jnp.where(level == levels, cluster[one, :].astype(jnp.float32), column)
        column = jnp.where(level == levels + 1, strength[one, :], column)
        base[2 + x] = column
        packed = jnp.where(pair == x, pltpu.roll(column, 2 * x, 1), packed)
        faces = face_y[1 + x]
        packed = jnp.where(pair == width + x, pltpu.roll(faces, 2 * (width + x), 1), packed)
        return packed

    packed = jnp.zeros((padded, lanes), jnp.float32)
    for x in (0, 1, width - 2, width - 1):
        packed = prepare(x, packed)
    pl.semaphore_wait(barrier, len(partners))
    copies_x = [
        send(base.at[pl.ds(width, 2)], base.at[pl.ds(0, 2)], 1, 0),
        send(base.at[pl.ds(2, 2)], base.at[pl.ds(width + 2, 2)], -1, 0),
        send(face_x.at[pl.ds(width, 2)], face_x.at[pl.ds(0, 2)], 1, 0),
        send(face_x.at[2], face_x.at[width + 2], -1, 0),
        send(face_y.at[width], face_y.at[0], 1, 0),
        send(face_y.at[1], face_y.at[width + 1], -1, 0),
    ]
    packed = lax.fori_loop(2, width - 2, prepare, packed, unroll=True)
    pack_a[0] = packed
    near, far = [], []
    for dt, ds in partners:
        if ds != 0:
            there = slot_of(-dt, n_t) * ny + slot_of(-ds, n_s)
            copy = send(pack_a.at[0], pack_a.at[there], dt, ds)
            (far if dt else near).append(copy)
    loads[7].wait()
    loads[8].wait()
    column, row = divmod_const(cells[...], n_s * lanes)
    tile, in_tile = divmod_const(column, width)
    block, in_block = divmod_const(row, lanes)
    step_t = tile - me_t
    step_t = jnp.where(step_t < 0, step_t + n_t, step_t)
    step_t = jnp.where(step_t > 1, 2, step_t)
    step_s = block - me_s
    step_s = jnp.where(step_s < 0, step_s + ny, step_s)
    table_row = (step_t * ny + step_s) * width + in_tile
    slots, elements = cells.shape
    lane_of = lax.broadcasted_iota(jnp.int32, (lanes, elements), 0)
    row_of = lax.broadcasted_iota(jnp.int32, (nx * ny * width, elements), 0)
    for k in range(slots):
        columns[k] = jnp.where(lane_of == in_block[k : k + 1], 1.0, 0.0).astype(jnp.bfloat16)

    for copy in near:
        copy.wait()

    odd = (lane & 1) == 1
    has_south = jnp.where(me_s > 0, 1.0, 0.0)
    has_north = jnp.where(me_s < n_s - 1, 1.0, 0.0)

    def merged(pack, dt):
        row = slot_of(dt, n_t) * ny
        south = pltpu.roll(pack[row + slot_of(-1, n_s)], 2, 1) * has_south
        north = pack[row + slot_of(1, n_s)] * has_north
        return jnp.where(odd, south, north)

    def edges(pack, at, value):
        seam = pltpu.roll(pack, lanes - 1 - 2 * at, 1)
        rows = lane[0 : value.shape[0]]
        north = jnp.where(rows == lanes - 1, seam, pltpu.roll(value, lanes - 1, 1))
        south = jnp.where(rows == 0, seam, pltpu.roll(value, 1, 1))
        return north, south

    seam_a = merged(pack_a, 0)
    first_id = (me_a * adjoints).astype(jnp.float32)

    def advance(x, seam, at):
        flow_y = face_y[1 + x]
        _, flow_south = edges(seam, width + at, flow_y)
        east_rate = jnp.maximum(face_x[2 + x], 0.0)
        west_rate = jnp.minimum(face_x[1 + x], 0.0)
        north_rate = jnp.maximum(flow_y, 0.0)
        south_rate = jnp.minimum(flow_south, 0.0)
        center_rate = 1.0 - east_rate + west_rate - north_rate + south_rate
        center, east, west = base[2 + x], base[3 + x], base[1 + x]
        north, south = edges(seam, at, center)
        terms = [
            (center * center_rate, center),
            (east * east_rate, east),
            (-west * west_rate, west),
            (north * north_rate, north),
            (-south * south_rate, south),
        ]
        values = []
        for a in range(adjoints):
            total = None
            for product, source in terms:
                ids = source[levels : levels + 1, :]
                chosen = jnp.where(ids == first_id + a, 1.0, 0.0)
                part = product * chosen
                total = part if total is None else total + part
            values.append(total)
        mixed = mix(jnp.concatenate(values, axis=1))
        fraction = center[levels + 1 : levels + 2, :]
        results = []
        for a in range(adjoints):
            value = values[a]
            value = value + fraction * (mixed[:, a * lanes : (a + 1) * lanes] - value)
            state[1 + x, a] = value
            results.append(value)
        return results

    def inside(x, packed):
        for a, value in enumerate(advance(x, seam_a, x)):
            at = a * width + x
            packed = jnp.where(pair == at, pltpu.roll(value, 2 * at, 1), packed)
        return packed

    packed = jnp.zeros((padded, lanes), jnp.float32)
    packed = lax.fori_loop(1, width - 1, inside, packed, unroll=True)
    for copy in copies_x:
        copy.wait()
    packed = inside(0, packed)
    packed = inside(width - 1, packed)
    pack_b[0] = packed
    copies = [
        send(pack_b.at[0], pack_b.at[slot_of(-ds, n_s)], 0, ds) for ds in offsets(n_s) if ds != 0
    ]
    for copy in far:
        copy.wait()
    advance(-1, merged(pack_a, -1), width - 1)
    advance(width, merged(pack_a, 1), 0)
    for k in range(slots):
        shares[k] = jnp.where(row_of == table_row[k : k + 1], weights[k : k + 1], 0.0)
    for copy in copies:
        copy.wait()
    seam_b = merged(pack_b, 0)

    stores = []

    def transport(low, high):
        top = min(high, levels)

        def along(x, carry):
            flow_y = face_y[1 + x, low:high]
            _, flow_south = edges(seam_a[low:high], width + x, flow_y)
            east_rate = jnp.maximum(face_x[2 + x, low:high], 0.0)
            west_rate = jnp.minimum(face_x[1 + x, low:high], 0.0)
            north_rate = jnp.maximum(flow_y, 0.0)
            south_rate = jnp.minimum(flow_south, 0.0)
            center_rate = 1.0 - east_rate + west_rate - north_rate + south_rate
            for a in range(adjoints):
                center = state[1 + x, a, low:high]
                north, south = edges(seam_b[low:high], a * width + x, center)
                value = (
                    center * center_rate
                    + east_rate * state[2 + x, a, low:high]
                    - west_rate * state[x, a, low:high]
                    + north_rate * north
                    - south_rate * south
                )
                rows = pl.ds((a * levels + low) * width + x, top - low, stride=width)
                held[rows, :] = value[0 : top - low, :]
                if low == 0:
                    table[0, pl.ds(a * width + x, 1), :] = value[0:1, :]
            return carry

        lax.fori_loop(0, width, along, 0, unroll=True)

    def store(low, high):
        top = min(high, levels)
        for a in range(adjoints):
            rows = pl.ds((a * levels + low) * width, (top - low) * width)
            copy = pltpu.make_async_copy(held.at[rows], field.at[rows], store_sem.at[len(stores)])
            copy.start()
            stores.append(copy)

    transport(0, 8)
    near, far = [], []
    for dt, ds in sorted(partners, key=lambda partner: partner[0] == 0):
        there = slot_of(-dt, n_t) * ny + slot_of(-ds, n_s)
        (far if dt else near).append(send(table.at[0], table.at[there], dt, ds))
    store(0, 8)
    for low in range(8, padded, 8):
        transport(low, low + 8)
        store(low, low + 8)

    chunk = 2 * lanes if elements % (2 * lanes) == 0 else lanes

    def gather(blocks, start):
        surface = table[blocks[0] : blocks[-1] + 1].reshape(len(blocks) * adjoints * width, lanes)
        surface = jnp.concatenate(split(surface), axis=1).astype(jnp.bfloat16)
        for c in range(elements // chunk):
            span = slice(c * chunk, (c + 1) * chunk)
            totals = [jnp.zeros((8, chunk), jnp.float32)] * adjoints
            for k in range(slots):
                chosen = columns[k, :, span]
                chosen = jnp.concatenate([chosen, chosen], axis=0)
                lines = jnp.dot(surface, chosen, preferred_element_type=jnp.float32)
                for a in range(adjoints):
                    for i, block in enumerate(blocks):
                        for x in range(0, width, 8):
                            line = (i * adjoints + a) * width + x
                            mine = block * width + x
                            totals[a] += lines[line : line + 8] * shares[k, mine : mine + 8, span]
            for a in range(adjoints):
                part = jnp.sum(totals[a], axis=0, keepdims=True)
                if not start:
                    part = part + sensed[a : a + 1, span]
                sensed[a : a + 1, span] = part

    for copy in near:
        copy.wait()
    gather(range(ny), True)
    for copy in far:
        copy.wait()
    gather(range(ny, nx * ny), False)
    for copy in stores:
        copy.wait()


def pass_body(adjoints, field, sensed, field_out, sensed_out, held, load_sem, store_sem):
    sensed_out[...] = sensed[...]
    share = field.shape[0] // adjoints
    loads, stores = [], []
    for a in range(adjoints):
        rows = pl.ds(a * share, share)
        loads.append(pltpu.make_async_copy(field.at[rows], held.at[rows], load_sem.at[a]))
        stores.append(pltpu.make_async_copy(held.at[rows], field_out.at[rows], store_sem.at[a]))
        loads[a].start()
    for load, store in zip(loads, stores):
        load.wait()
        store.start()
    for store in stores:
        store.wait()


def body(
    innovation,
    cluster,
    kernel,
    wind_x,
    wind_y,
    conv_strength,
    conv_matrix,
    margin_cell,
    margin_weight,
):
    levels, width, lanes = kernel.shape
    n_t, n_s = lax.axis_size("tiles"), lax.axis_size("sub")
    adjoints = ADJ // lax.axis_size("adj")
    elements, slots = margin_cell.shape
    padded = 8 * pl.cdiv(levels + 2, 8)
    depth = 128 * pl.cdiv(3 * padded, 128)
    nx, ny = min(3, n_t), min(3, n_s)
    n_sems = 6 + 2 * (nx * ny - 1) - (nx - 1) + ny - 1
    anywhere = pl.BlockSpec(memory_space=pl.ANY)
    vmem = pl.BlockSpec(memory_space=pltpu.VMEM)
    limit = 60 * 1024 * 1024
    operands = (
        innovation,
        cluster,
        kernel.reshape(levels * width, lanes),
        wind_x.reshape(levels * width, lanes),
        wind_y.reshape(levels * width, lanes),
        conv_strength,
        conv_matrix,
        margin_cell.T,
        margin_weight.T,
    )
    field_shape = jax.ShapeDtypeStruct((adjoints * levels * width, lanes), jnp.float32)
    sensed_shape = jax.ShapeDtypeStruct((adjoints, elements), jnp.float32)
    field, sensed = pl.pallas_call(
        functools.partial(kernel_body, (levels, width, adjoints, n_t, n_s)),
        out_shape=(field_shape, sensed_shape),
        in_specs=[anywhere] * len(operands),
        out_specs=(anywhere, vmem),
        scratch_shapes=[pltpu.VMEM(x.shape, x.dtype) for x in operands]
        + [
            pltpu.VMEM((width + 4, padded, lanes), jnp.float32),
            pltpu.VMEM((width + 3, padded, lanes), jnp.float32),
            pltpu.VMEM((width + 2, padded, lanes), jnp.float32),
            pltpu.VMEM((nx * ny, padded, lanes), jnp.float32),
            pltpu.VMEM((ny, padded, lanes), jnp.float32),
            pltpu.VMEM((width + 2, adjoints, padded, lanes), jnp.float32),
            pltpu.VMEM((nx * ny, adjoints * width, lanes), jnp.float32),
            pltpu.VMEM(field_shape.shape, jnp.float32),
            pltpu.VMEM((depth, depth), jnp.float32),
            pltpu.VMEM((slots, lanes, elements), jnp.bfloat16),
            pltpu.VMEM((slots, nx * ny * width, elements), jnp.float32),
            pltpu.SemaphoreType.DMA((n_sems,)),
            pltpu.SemaphoreType.DMA((n_sems,)),
            pltpu.SemaphoreType.DMA((len(operands),)),
            pltpu.SemaphoreType.DMA((adjoints * padded // 8,)),
        ],
        compiler_params=pltpu.CompilerParams(
            collective_id=0, has_side_effects=True, vmem_limit_bytes=limit
        ),
    )(*operands)
    field, sensed = pl.pallas_call(
        functools.partial(pass_body, adjoints),
        out_shape=(field_shape, sensed_shape),
        in_specs=[anywhere, vmem],
        out_specs=(anywhere, vmem),
        scratch_shapes=[
            pltpu.VMEM(field_shape.shape, jnp.float32),
            pltpu.SemaphoreType.DMA((adjoints,)),
            pltpu.SemaphoreType.DMA((adjoints,)),
        ],
        compiler_params=pltpu.CompilerParams(vmem_limit_bytes=limit),
    )(field, sensed)
    return field.reshape(adjoints, levels, width, lanes), sensed


def solution(mesh):
    in_specs = (
        P(("groups", "tiles"), "sub"),
        P(("groups", "tiles"), "sub"),
        P(None, "tiles", "sub"),
        P(None, "tiles", "sub"),
        P(None, "tiles", "sub"),
        P("tiles", "sub"),
        P(),
        P(("tiles", "sub"), None),
        P(("tiles", "sub"), None),
    )
    out_specs = (P(("groups", "adj"), None, "tiles", "sub"), P(("groups", "adj"), ("tiles", "sub")))
    return jax.shard_map(body, mesh=mesh, in_specs=in_specs, out_specs=out_specs, check_vma=False)
```

```python
import functools

import jax
import jax.numpy as jnp
from jax import lax
from jax.experimental import pallas as pl
from jax.experimental.pallas import tpu as pltpu
from jax.sharding import PartitionSpec as P

ADJ = 8
NSTEP = 2
MESH = pl.DeviceIdType.MESH


def offsets(count):
    return [0, 1, -1][: min(3, count)]


def slot_of(offset, count):
    return offset % min(3, count)


def divmod_const(value, number):
    if number & (number - 1) == 0:
        return value >> (number.bit_length() - 1), value & (number - 1)
    return value // number, value % number


def split(value):
    high = value.astype(jnp.bfloat16).astype(jnp.float32)
    return high, value - high


def stacked(value, depth):
    high, low = split(value)
    rows, lanes = value.shape
    parts = [high, low, high]
    if depth > 3 * rows:
        parts.append(jnp.zeros((depth - 3 * rows, lanes), jnp.float32))
    return jnp.concatenate(parts, axis=0).astype(jnp.bfloat16)


def kernel_body(
    dims,
    *refs,
):
    sources, (field, sensed), scratch = refs[:9], refs[9:11], refs[11:]
    arrivals, scratch = scratch[:9], scratch[9:]
    innovation, cluster, kernel, wind_x, wind_y, strength, matrix, cells, weights = arrivals
    (
        base,
        face_x,
        face_y,
        pack_a,
        pack_b,
        state,
        table,
        held,
        square,
        columns,
        shares,
        send_sem,
        recv_sem,
        load_sem,
        store_sem,
    ) = scratch
    levels, width, adjoints, n_t, n_s = dims
    padded = base.shape[1]
    lanes = base.shape[2]
    depth = square.shape[0]
    me_g = lax.axis_index("groups")
    me_t = lax.axis_index("tiles")
    me_s = lax.axis_index("sub")
    me_a = lax.axis_index("adj")
    nx, ny = min(3, n_t), min(3, n_s)

    def device(dt, ds):
        return (me_g, lax.rem(me_t + dt + n_t, n_t), lax.rem(me_s + ds + n_s, n_s), me_a)

    partners = [(dt, ds) for dt in offsets(n_t) for ds in offsets(n_s) if (dt, ds) != (0, 0)]
    barrier = pltpu.get_barrier_semaphore()
    for dt, ds in partners:
        pl.semaphore_signal(barrier, inc=1, device_id=device(dt, ds), device_id_type=MESH)
    loads = [
        pltpu.make_async_copy(source, arrival, load_sem.at[i])
        for i, (source, arrival) in enumerate(zip(sources, arrivals))
    ]
    for i in (6, 2, 0, 1, 5, 3, 4, 7, 8):
        loads[i].start()

    count = [0]

    def send(src, dst, dt, ds):
        at = count[0]
        count[0] += 1
        copy = pltpu.make_async_remote_copy(
            src_ref=src,
            dst_ref=dst,
            send_sem=send_sem.at[at],
            recv_sem=recv_sem.at[at],
            device_id=device(dt, ds),
            device_id_type=MESH,
        )
        copy.start()
        return copy

    square[...] = jnp.zeros_like(square)
    loads[6].wait()
    square[0:levels, 0:levels] = matrix[...]
    high, low = split(square[...].T)
    mixer = high + pltpu.roll(high, padded, 1) + pltpu.roll(low, 2 * padded, 1)
    mixer = mixer[0:padded].astype(jnp.bfloat16)

    def mix(value):
        return jnp.dot(mixer, stacked(value, depth), preferred_element_type=jnp.float32)

    lane = lax.broadcasted_iota(jnp.int32, (padded, lanes), 1)
    pair = ((lane + 1) & (lanes - 1)) >> 1
    level = lax.broadcasted_iota(jnp.int32, (padded, lanes), 0)

    last = levels // 8 * 8
    for load in loads[:6]:
        load.wait()

    def prepare(x, packed):
        rows = pl.ds(x, levels, stride=width)
        empty = jnp.zeros((padded - last, lanes), jnp.float32)
        face_x[2 + x, last:padded, :] = empty
        face_y[1 + x, last:padded, :] = empty
        base[2 + x, last:padded, :] = empty
        face_x[2 + x, 0:levels, :] = wind_x[rows, :]
        face_y[1 + x, 0:levels, :] = wind_y[rows, :]
        base[2 + x, 0:levels, :] = kernel[rows, :]
        column = base[2 + x]
        one = pl.ds(x, 1)
        mixed = mix(column)
        column = (column + strength[one, :] * (mixed - column)) * innovation[one, :]
        column = jnp.where(level == levels, cluster[one, :].astype(jnp.float32), column)
        column = jnp.where(level == levels + 1, strength[one, :], column)
        base[2 + x] = column
        packed = jnp.where(pair == x, pltpu.roll(column, 2 * x, 1), packed)
        faces = face_y[1 + x]
        packed = jnp.where(pair == width + x, pltpu.roll(faces, 2 * (width + x), 1), packed)
        return packed

    packed = jnp.zeros((padded, lanes), jnp.float32)
    for x in (0, 1, width - 2, width - 1):
        packed = prepare(x, packed)
    pl.semaphore_wait(barrier, len(partners))
    copies_x = [
        send(base.at[pl.ds(width, 2)], base.at[pl.ds(0, 2)], 1, 0),
        send(base.at[pl.ds(2, 2)], base.at[pl.ds(width + 2, 2)], -1, 0),
        send(face_x.at[pl.ds(width, 2)], face_x.at[pl.ds(0, 2)], 1, 0),
        send(face_x.at[2], face_x.at[width + 2], -1, 0),
        send(face_y.at[width], face_y.at[0], 1, 0),
        send(face_y.at[1], face_y.at[width + 1], -1, 0),
    ]
    packed = lax.fori_loop(2, width - 2, prepare, packed, unroll=True)
    pack_a[0] = packed
    near, far = [], []
    for dt, ds in partners:
        if ds != 0:
            there = slot_of(-dt, n_t) * ny + slot_of(-ds, n_s)
            copy = send(pack_a.at[0], pack_a.at[there], dt, ds)
            (far if dt else near).append(copy)
    loads[7].wait()
    loads[8].wait()
    column, row = divmod_const(cells[...], n_s * lanes)
    tile, in_tile = divmod_const(column, width)
    block, in_block = divmod_const(row, lanes)
    step_t = tile - me_t
    step_t = jnp.where(step_t < 0, step_t + n_t, step_t)
    step_t = jnp.where(step_t > 1, 2, step_t)
    step_s = block - me_s
    step_s = jnp.where(step_s < 0, step_s + ny, step_s)
    table_row = (step_t * ny + step_s) * width + in_tile
    slots, elements = cells.shape
    lane_of = lax.broadcasted_iota(jnp.int32, (lanes, elements), 0)
    row_of = lax.broadcasted_iota(jnp.int32, (nx * ny * width, elements), 0)
    for k in range(slots):
        columns[k] = jnp.where(lane_of == in_block[k : k + 1], 1.0, 0.0).astype(jnp.bfloat16)

    for copy in near:
        copy.wait()

    odd = (lane & 1) == 1
    has_south = jnp.where(me_s > 0, 1.0, 0.0)
    has_north = jnp.where(me_s < n_s - 1, 1.0, 0.0)

    def merged(pack, dt):
        row = slot_of(dt, n_t) * ny
        south = pltpu.roll(pack[row + slot_of(-1, n_s)], 2, 1) * has_south
        north = pack[row + slot_of(1, n_s)] * has_north
        return jnp.where(odd, south, north)

    def edges(pack, at, value):
        seam = pltpu.roll(pack, lanes - 1 - 2 * at, 1)
        rows = lane[0 : value.shape[0]]
        north = jnp.where(rows == lanes - 1, seam, pltpu.roll(value, lanes - 1, 1))
        south = jnp.where(rows == 0, seam, pltpu.roll(value, 1, 1))
        return north, south

    seam_a = merged(pack_a, 0)
    first_id = (me_a * adjoints).astype(jnp.float32)

    def advance(x, seam, at):
        flow_y = face_y[1 + x]
        _, flow_south = edges(seam, width + at, flow_y)
        east_rate = jnp.maximum(face_x[2 + x], 0.0)
        west_rate = jnp.minimum(face_x[1 + x], 0.0)
        north_rate = jnp.maximum(flow_y, 0.0)
        south_rate = jnp.minimum(flow_south, 0.0)
        center_rate = 1.0 - east_rate + west_rate - north_rate + south_rate
        center, east, west = base[2 + x], base[3 + x], base[1 + x]
        north, south = edges(seam, at, center)
        terms = [
            (center * center_rate, center),
            (east * east_rate, east),
            (-west * west_rate, west),
            (north * north_rate, north),
            (-south * south_rate, south),
        ]
        values = []
        for a in range(adjoints):
            total = None
            for product, source in terms:
                ids = source[levels : levels + 1, :]
                chosen = jnp.where(ids == first_id + a, 1.0, 0.0)
                part = product * chosen
                total = part if total is None else total + part
            values.append(total)
        mixed = mix(jnp.concatenate(values, axis=1))
        fraction = center[levels + 1 : levels + 2, :]
        results = []
        for a in range(adjoints):
            value = values[a]
            value = value + fraction * (mixed[:, a * lanes : (a + 1) * lanes] - value)
            state[1 + x, a] = value
            results.append(value)
        return results

    def inside(x, packed):
        for a, value in enumerate(advance(x, seam_a, x)):
            at = a * width + x
            packed = jnp.where(pair == at, pltpu.roll(value, 2 * at, 1), packed)
        return packed

    packed = jnp.zeros((padded, lanes), jnp.float32)
    packed = lax.fori_loop(1, width - 1, inside, packed, unroll=True)
    for copy in copies_x:
        copy.wait()
    packed = inside(0, packed)
    packed = inside(width - 1, packed)
    pack_b[0] = packed
    copies = [
        send(pack_b.at[0], pack_b.at[slot_of(-ds, n_s)], 0, ds) for ds in offsets(n_s) if ds != 0
    ]
    for copy in far:
        copy.wait()
    advance(-1, merged(pack_a, -1), width - 1)
    advance(width, merged(pack_a, 1), 0)
    for k in range(slots):
        shares[k] = jnp.where(row_of == table_row[k : k + 1], weights[k : k + 1], 0.0)
    for copy in copies:
        copy.wait()
    seam_b = merged(pack_b, 0)

    stores = []

    def transport(low, high):
        top = min(high, levels)

        def along(x, carry):
            flow_y = face_y[1 + x, low:high]
            _, flow_south = edges(seam_a[low:high], width + x, flow_y)
            east_rate = jnp.maximum(face_x[2 + x, low:high], 0.0)
            west_rate = jnp.minimum(face_x[1 + x, low:high], 0.0)
            north_rate = jnp.maximum(flow_y, 0.0)
            south_rate = jnp.minimum(flow_south, 0.0)
            center_rate = 1.0 - east_rate + west_rate - north_rate + south_rate
            for a in range(adjoints):
                center = state[1 + x, a, low:high]
                north, south = edges(seam_b[low:high], a * width + x, center)
                value = (
                    center * center_rate
                    + east_rate * state[2 + x, a, low:high]
                    - west_rate * state[x, a, low:high]
                    + north_rate * north
                    - south_rate * south
                )
                rows = pl.ds((a * levels + low) * width + x, top - low, stride=width)
                held[rows, :] = value[0 : top - low, :]
                if low == 0:
                    table[0, pl.ds(a * width + x, 1), :] = value[0:1, :]
            return carry

        lax.fori_loop(0, width, along, 0, unroll=True)

    def store(low, high):
        top = min(high, levels)
        for a in range(adjoints):
            rows = pl.ds((a * levels + low) * width, (top - low) * width)
            copy = pltpu.make_async_copy(held.at[rows], field.at[rows], store_sem.at[len(stores)])
            copy.start()
            stores.append(copy)

    transport(0, 8)
    near, far = [], []
    for dt, ds in sorted(partners, key=lambda partner: partner[0] == 0):
        there = slot_of(-dt, n_t) * ny + slot_of(-ds, n_s)
        (far if dt else near).append(send(table.at[0], table.at[there], dt, ds))
    store(0, 8)
    for low in range(8, padded, 8):
        transport(low, low + 8)
        store(low, low + 8)

    chunk = 2 * lanes if elements % (2 * lanes) == 0 else lanes

    def gather(blocks, start):
        surface = table[blocks[0] : blocks[-1] + 1].reshape(len(blocks) * adjoints * width, lanes)
        surface = jnp.concatenate(split(surface), axis=1).astype(jnp.bfloat16)
        for c in range(elements // chunk):
            span = slice(c * chunk, (c + 1) * chunk)
            totals = [jnp.zeros((8, chunk), jnp.float32)] * adjoints
            for k in range(slots):
                chosen = columns[k, :, span]
                chosen = jnp.concatenate([chosen, chosen], axis=0)
                lines = jnp.dot(surface, chosen, preferred_element_type=jnp.float32)
                for a in range(adjoints):
                    for i, block in enumerate(blocks):
                        for x in range(0, width, 8):
                            line = (i * adjoints + a) * width + x
                            mine = block * width + x
                            totals[a] += lines[line : line + 8] * shares[k, mine : mine + 8, span]
            for a in range(adjoints):
                part = jnp.sum(totals[a], axis=0, keepdims=True)
                if not start:
                    part = part + sensed[a : a + 1, span]
                sensed[a : a + 1, span] = part

    for copy in near:
        copy.wait()
    gather(range(ny), True)
    for copy in far:
        copy.wait()
    gather(range(ny, nx * ny), False)
    for copy in stores:
        copy.wait()


def pass_body(parts, field, sensed, field_out, sensed_out, field_held, sensed_held, load_sem, store_sem):
    share = field.shape[0] // parts
    pieces = [pl.ds(part * share, share) for part in range(parts)]
    loads = [(field.at[piece], field_held.at[piece]) for piece in pieces] + [(sensed, sensed_held)]
    stores = [(field_held.at[piece], field_out.at[piece]) for piece in pieces]
    stores.append((sensed_held, sensed_out))
    loads = [pltpu.make_async_copy(*ends, load_sem.at[i]) for i, ends in enumerate(loads)]
    stores = [pltpu.make_async_copy(*ends, store_sem.at[i]) for i, ends in enumerate(stores)]
    for load in loads:
        load.start()
    for load, store in zip(loads, stores):
        load.wait()
        store.start()
    for store in stores:
        store.wait()


def body(
    innovation,
    cluster,
    kernel,
    wind_x,
    wind_y,
    conv_strength,
    conv_matrix,
    margin_cell,
    margin_weight,
):
    levels, width, lanes = kernel.shape
    n_t, n_s = lax.axis_size("tiles"), lax.axis_size("sub")
    adjoints = ADJ // lax.axis_size("adj")
    elements, slots = margin_cell.shape
    padded = 8 * pl.cdiv(levels + 2, 8)
    depth = 128 * pl.cdiv(3 * padded, 128)
    nx, ny = min(3, n_t), min(3, n_s)
    n_sems = 6 + 2 * (nx * ny - 1) - (nx - 1) + ny - 1
    anywhere = pl.BlockSpec(memory_space=pl.ANY)
    vmem = pl.BlockSpec(memory_space=pltpu.VMEM)
    limit = 60 * 1024 * 1024
    operands = (
        innovation,
        cluster,
        kernel.reshape(levels * width, lanes),
        wind_x.reshape(levels * width, lanes),
        wind_y.reshape(levels * width, lanes),
        conv_strength,
        conv_matrix,
        margin_cell.T,
        margin_weight.T,
    )
    field_shape = jax.ShapeDtypeStruct((adjoints * levels * width, lanes), jnp.float32)
    sensed_shape = jax.ShapeDtypeStruct((adjoints, elements), jnp.float32)
    field, sensed = pl.pallas_call(
        functools.partial(kernel_body, (levels, width, adjoints, n_t, n_s)),
        out_shape=(field_shape, sensed_shape),
        in_specs=[anywhere] * len(operands),
        out_specs=(anywhere, vmem),
        scratch_shapes=[pltpu.VMEM(x.shape, x.dtype) for x in operands]
        + [
            pltpu.VMEM((width + 4, padded, lanes), jnp.float32),
            pltpu.VMEM((width + 3, padded, lanes), jnp.float32),
            pltpu.VMEM((width + 2, padded, lanes), jnp.float32),
            pltpu.VMEM((nx * ny, padded, lanes), jnp.float32),
            pltpu.VMEM((ny, padded, lanes), jnp.float32),
            pltpu.VMEM((width + 2, adjoints, padded, lanes), jnp.float32),
            pltpu.VMEM((nx * ny, adjoints * width, lanes), jnp.float32),
            pltpu.VMEM(field_shape.shape, jnp.float32),
            pltpu.VMEM((depth, depth), jnp.float32),
            pltpu.VMEM((slots, lanes, elements), jnp.bfloat16),
            pltpu.VMEM((slots, nx * ny * width, elements), jnp.float32),
            pltpu.SemaphoreType.DMA((n_sems,)),
            pltpu.SemaphoreType.DMA((n_sems,)),
            pltpu.SemaphoreType.DMA((len(operands),)),
            pltpu.SemaphoreType.DMA((adjoints * padded // 8,)),
        ],
        compiler_params=pltpu.CompilerParams(
            collective_id=0, has_side_effects=True, vmem_limit_bytes=limit
        ),
    )(*operands)
    parts = 2 * adjoints
    field, sensed = pl.pallas_call(
        functools.partial(pass_body, parts),
        out_shape=(field_shape, sensed_shape),
        in_specs=[anywhere, anywhere],
        out_specs=(anywhere, anywhere),
        scratch_shapes=[
            pltpu.VMEM(field_shape.shape, jnp.float32),
            pltpu.VMEM(sensed_shape.shape, jnp.float32),
            pltpu.SemaphoreType.DMA((parts + 1,)),
            pltpu.SemaphoreType.DMA((parts + 1,)),
        ],
        compiler_params=pltpu.CompilerParams(vmem_limit_bytes=limit),
    )(field, sensed)
    return field.reshape(adjoints, levels, width, lanes), sensed


def solution(mesh):
    in_specs = (
        P(("groups", "tiles"), "sub"),
        P(("groups", "tiles"), "sub"),
        P(None, "tiles", "sub"),
        P(None, "tiles", "sub"),
        P(None, "tiles", "sub"),
        P("tiles", "sub"),
        P(),
        P(("tiles", "sub"), None),
        P(("tiles", "sub"), None),
    )
    out_specs = (P(("groups", "adj"), None, "tiles", "sub"), P(("groups", "adj"), ("tiles", "sub")))
    return jax.shard_map(body, mesh=mesh, in_specs=in_specs, out_specs=out_specs, check_vma=False)
```
